512 devices in a mesh: cache: 64 (over x, z, core), tp: 8 (over y).
Axes of the slice: x: 4, y: 8, z: 8, core: 2. Of those that a mesh axis runs over, the one named last changes fastest.
Arguments:
- query: bfloat16 [64, 256, 8192], P('cache', 'tp')
- qkeys: bfloat16 [64, 256, 1024], P('cache', 'tp')
- qvalues: bfloat16 [64, 256, 1024], P('cache', 'tp'), may hold values from -6 to 6
- cache_keys: bfloat16 [256, 512, 1024], P('cache', None, 'tp'), may hold values from -6 to 6
- cache_values: bfloat16 [256, 512, 1024], P('cache', None, 'tp'), may hold values from -6 to 6
- lists: int32 [64, 8], P('cache'), may hold values from 0 to 255, all different within a row
Outputs:
- attended: bfloat16 [64, 256, 8192], P('cache', 'tp')
The draws below stay inside these ranges and needn't reach their ends.
Inputs may be any that keep to these rules, and one draw needn't show every extreme that they name: `lists`: each row names 8 different passages; every passage is named by some request.
All inputs are finite; a program needn't handle non-finite values.
Results may differ from the reference program's by a relative error of at most 0.0046.
Values may be sent and summed in bfloat16 or wider, within the bound.
No kernel may reach another device: no remote copies, remote signals or barrier semaphores. Data moves between devices by JAX's collectives and lax.ppermute only.
A program may use at most 64 MiB of HBM per device.

```python
import jax
import jax.numpy as jnp
from jax import lax

HEADS = 64
KVH = 8
HD = 128
PLEN = 512
TOPP = 8
QLEN = 256
GROUP = 8
PASSAGES = 256
REQUESTS = 64


def shared_rows(key):
    noise = jax.random.normal(jax.random.fold_in(key, 11), (REQUESTS, QLEN, KVH, HD), jnp.float32)
    return noise


def draw_qkeys(key, part):
    noise = shared_rows(key)
    values = noise
    return values.reshape(REQUESTS, QLEN, KVH * HD).astype(jnp.bfloat16)


def draw_query(key, part):
    key = jax.random.fold_in(key, 3)
    base = jax.random.normal(key, (REQUESTS, QLEN, KVH, GROUP, HD), jnp.float32)
    return base.reshape(REQUESTS, QLEN, HEADS * HD).astype(jnp.bfloat16)


def levels(own_key, shape, pieces, least, largest):
    factor_of = 1.0
    for axis_at, parts in pieces:
        draws = jax.random.uniform(jax.random.fold_in(jax.random.fold_in(own_key, 6), axis_at), (parts,), jnp.float32, least / len(pieces), largest / len(pieces))
        factor_of = factor_of * jnp.repeat(jnp.exp(draws), shape[axis_at] // parts).reshape((-1,) + (1,) * (len(shape) - 1 - axis_at))
    return factor_of


def picks_of(own_key, rows, number_of, top, lift):
    sequence = jax.random.permutation(jax.random.fold_in(own_key, 1), number_of)
    boost = sequence
    for power in range(3):
        boost = boost * boost // number_of
    boost = boost * lift // number_of
    tickets = jax.random.randint(jax.random.fold_in(own_key, 2), (rows, number_of), 0, 4096) + boost
    sure = jax.random.permutation(jax.random.fold_in(own_key, 3), rows)[jnp.arange(number_of) % rows]
    tickets = jnp.where(jnp.arange(rows)[:, None] == sure[None, :], 1 << 14, tickets)
    priority = tickets * number_of + jnp.arange(number_of)
    return lax.top_k(priority.astype(jnp.int32), top)[1].astype(jnp.int32)


def scatter_about(own_key, extent, spread, most, shards=(), dtype=jnp.bfloat16):
    values = spread * jax.random.normal(own_key, extent, jnp.float32)
    if shards:
        values = values * levels(own_key, extent, shards, -0.22, 0.18)
    return jnp.clip(values, -most, most).astype(dtype)


def setup_inputs(seed: int = 0) -> dict:
    splits = jax.random.split(jax.random.key(seed), 7)
    return {
        "query": draw_query(jax.random.fold_in(splits[6], 71), 0),
        "qkeys": draw_qkeys(jax.random.fold_in(splits[6], 71), 0),
        "qvalues": scatter_about(splits[2], (REQUESTS, QLEN, KVH * HD), 1.0, 6.0, ((0, 64), (1, 8))),
        "cache_keys": scatter_about(splits[3], (PASSAGES, PLEN, KVH * HD), 1.0, 6.0, ((0, 64), (2, 8))),
        "cache_values": scatter_about(splits[4], (PASSAGES, PLEN, KVH * HD), 1.0, 6.0, ((0, 64), (2, 8))),
        "lists": picks_of(splits[5], REQUESTS, PASSAGES, TOPP, 512),
    }


NEG = -1e30


def block_part(queries, keys, values, mask):
    kv_count = queries.shape[0]
    head_dim = queries.shape[3]
    keys_h = keys.reshape(keys.shape[0], kv_count, head_dim).transpose(1, 0, 2)
    values_h = values.reshape(values.shape[0], kv_count, head_dim).transpose(1, 0, 2)
    scale = head_dim ** -0.5

    def one_head(items):
        query_h, key_h, value_h = items
        scores = jnp.einsum("gqd,nd->gqn", query_h.astype(jnp.float32), key_h.astype(jnp.float32)) * scale
        if mask is not None:
            scores = jnp.where(mask[None], scores, NEG)
        top = jnp.max(scores, axis=-1)
        weights = jnp.exp(scores - top[..., None])
        totals = jnp.sum(weights, axis=-1)
        rounded = weights.astype(jnp.bfloat16)
        output = jnp.einsum("gqn,nd->gqd", rounded.astype(jnp.float32), value_h.astype(jnp.float32))
        return output, top, totals

    return lax.map(one_head, (queries, keys_h, values_h))


def combine(own, outs_b, maxes, totals):
    own_out, own_max, own_tot = own
    top = jnp.maximum(own_max, jnp.max(maxes, axis=0))
    own_w = jnp.exp(own_max - top)
    block_w = jnp.exp(maxes - top[None])
    numer = own_out * own_w[..., None] + jnp.sum(outs_b * block_w[..., None], axis=0)
    denom = own_tot * own_w + jnp.sum(totals * block_w, axis=0)
    return (numer / denom[..., None]).astype(jnp.bfloat16)


def reference(query, qkeys, qvalues, cache_keys, cache_values, lists):
    def one_request(items):
        query_r, keys_r, values_r, list_r = items
        qlen = query_r.shape[0]
        queries = query_r.reshape(qlen, KVH, GROUP, HD).transpose(1, 2, 0, 3)
        causal = jnp.arange(qlen)[:, None] >= jnp.arange(qlen)[None, :]
        own = block_part(queries, keys_r, values_r, causal)
        picked_k = jnp.take(cache_keys, list_r.astype(jnp.int32), axis=0)
        picked_v = jnp.take(cache_values, list_r.astype(jnp.int32), axis=0)
        outs_b, maxes, totals = lax.map(lambda kv: block_part(queries, kv[0], kv[1], None), (picked_k, picked_v))
        merged = combine(own, outs_b, maxes, totals)
        return merged.transpose(2, 0, 1, 3).reshape(qlen, HEADS * HD)

    return lax.map(one_request, (query, qkeys, qvalues, lists))
```

```python
import functools

import jax
import jax.numpy as jnp
from jax import lax
from jax.experimental import pallas as pl
from jax.experimental.pallas import tpu as pltpu
from jax.sharding import PartitionSpec as P

HD = 128
ROWS = 16
LOG2E = 1.4426950408889634
VMEM = pltpu.CompilerParams(vmem_limit_bytes=48 * 1024 * 1024)


def whole(shape):
    return pl.BlockSpec(shape, lambda *_: (0,) * len(shape))


def cut_bands(cache_keys, cache_values, parts):
    owned, plen, width = cache_keys.shape
    half = parts // 2

    def kernel(k_ref, v_ref, out_ref):
        for i in range(owned):
            out_ref[:half, i] = k_ref[i].reshape(half, ROWS, width)
            out_ref[half:, i] = v_ref[i].reshape(half, ROWS, width)

    return pl.pallas_call(
        kernel,
        out_shape=jax.ShapeDtypeStruct((parts, owned, ROWS, width), cache_keys.dtype),
        compiler_params=VMEM,
        name="cut_bands",
    )(cache_keys, cache_values)


def gather_lists(lists, parts):
    seen, step = lists, 1
    while step < parts:
        order = [((d + step) % parts, d) for d in range(parts)]
        seen = jnp.concatenate([seen, lax.ppermute(seen, "cache", order)], axis=0)
        step *= 2
    return seen


def pick_rows(band, lists, me):
    parts, top = lists.shape
    width = band.shape[2]
    steps = 4
    share = parts // steps

    def kernel(me_ref, lists_ref, band_ref, out_ref):
        first = pl.program_id(0) * share

        def one(d, carry):
            row = lax.rem(first + d - me_ref[0] + parts, parts)
            for j in range(top):
                out_ref[d, j] = band_ref[lists_ref[row, j]]
            return carry

        lax.fori_loop(0, share, one, 0, unroll=2)

    return pl.pallas_call(
        kernel,
        grid_spec=pltpu.PrefetchScalarGridSpec(
            num_scalar_prefetch=2,
            grid=(steps,),
            in_specs=[whole(band.shape)],
            out_specs=pl.BlockSpec((share, top, ROWS, width), lambda s, *_: (s, 0, 0, 0)),
        ),
        out_shape=jax.ShapeDtypeStruct((parts, top, ROWS, width), band.dtype),
        compiler_params=VMEM,
        name="pick_rows",
    )(me, lists, band)


def cut_heads(query, qkeys, qvalues, me, tp):
    tokens, width = query.shape[0], query.shape[1] // tp
    small = qkeys.shape[1] // tp

    def kernel(me_ref, q_ref, k_ref, v_ref, *outs):
        for k in range(tp):
            to = lax.rem(me_ref[0] + k, tp)
            big = pl.ds(pl.multiple_of(to * width, width), width)
            own = pl.ds(pl.multiple_of(to * small, small), small)
            outs[k][:, :width] = q_ref[:, big]
            outs[k][:, width : width + small] = k_ref[:, own]
            outs[k][:, width + small :] = v_ref[:, own]

    total = width + 2 * small
    return pl.pallas_call(
        kernel,
        grid_spec=pltpu.PrefetchScalarGridSpec(
            num_scalar_prefetch=1,
            grid=(1,),
            in_specs=[whole(query.shape), whole(qkeys.shape), whole(qvalues.shape)],
            out_specs=[whole((tokens, total))] * tp,
        ),
        out_shape=[jax.ShapeDtypeStruct((tokens, total), query.dtype)] * tp,
        compiler_params=VMEM,
        name="cut_heads",
    )(me, query, qkeys, qvalues)


def attend(parts_q, received, me, group):
    tp = len(parts_q)
    tokens, total = parts_q[0].shape
    qlen = tp * tokens
    width = group * HD
    bands, top, rows, _ = received.shape
    half = bands // 2
    keys_n = half * top * rows
    per = 2
    chunk = 512
    factor = HD ** (-0.5) * LOG2E

    def kernel(me_ref, *refs):
        q_refs = refs[:tp]
        k_ref, v_ref, out_ref, scores, weights, values = refs[tp:]
        mine = me_ref[0]

        @pl.when(pl.program_id(0) == 0)
        def _():
            values[:, HD:] = jnp.ones((keys_n + qlen, HD), values.dtype)
            values[:keys_n, :HD] = v_ref[...].reshape(keys_n, HD)
            for k in range(tp):
                values[keys_n + k * tokens : keys_n + (k + 1) * tokens, :HD] = q_refs[k][:, width + HD :]

        def position(axis):
            index = lax.broadcasted_iota(jnp.int32, (qlen, qlen), axis)
            owner = lax.bitwise_and(mine - index // tokens + tp, tp - 1)
            return owner * tokens + lax.rem(index, tokens)

        sees = position(0) >= position(1)
        own_keys = jnp.concatenate([q_refs[k][:, width : width + HD] for k in range(tp)], axis=0)
        dims = (((1,), (1,)), ((), ()))
        for p in range(per):
            at = pl.ds(pl.multiple_of((pl.program_id(0) * per + p) * HD, HD), HD)
            q = jnp.concatenate([q_refs[k][:, at] for k in range(tp)], axis=0)
            s = lax.dot_general(q, own_keys, dims, preferred_element_type=jnp.float32)
            s = jnp.where(sees, s, -jnp.inf)
            scores[p, :, keys_n:] = s
            most = functools.reduce(jnp.maximum, [s[:, i : i + HD] for i in range(0, qlen, HD)])
            for c in range(0, keys_n, chunk):
                keys = k_ref[c // (top * rows) : (c + chunk) // (top * rows)].reshape(chunk, HD)
                s = lax.dot_general(q, keys, dims, preferred_element_type=jnp.float32)
                scores[p, :, c : c + chunk] = s
                most = functools.reduce(jnp.maximum, [s[:, i : i + HD] for i in range(0, chunk, HD)], most)
            m = jnp.max(most, axis=1, keepdims=True)
            for c in range(0, keys_n + qlen, 256):
                s = scores[p, :, c : c + 256]
                weights[p, :, c : c + 256] = jnp.exp2((s - m) * factor).astype(weights.dtype)
            o = jnp.dot(weights[p], values[...], preferred_element_type=jnp.float32)
            o = (o[:, :HD] / o[:, HD:]).astype(out_ref.dtype)
            for k in range(tp):
                owner = lax.bitwise_and(mine - k + tp, tp - 1)
                out_ref[owner, :, p * HD : (p + 1) * HD] = o[k * tokens : (k + 1) * tokens]

    return pl.pallas_call(
        kernel,
        grid_spec=pltpu.PrefetchScalarGridSpec(
            num_scalar_prefetch=1,
            grid=(group // per,),
            in_specs=[whole((tokens, total))] * tp
            + [
                pl.BlockSpec((half, top, rows, HD), lambda s, *_: (0, 0, 0, 0)),
                pl.BlockSpec((half, top, rows, HD), lambda s, *_: (1, 0, 0, 0)),
            ],
            out_specs=pl.BlockSpec((tp, tokens, per * HD), lambda s, *_: (0, 0, s)),
            scratch_shapes=[
                pltpu.VMEM((per, qlen, keys_n + qlen), jnp.float32),
                pltpu.VMEM((per, qlen, keys_n + qlen), jnp.bfloat16),
                pltpu.VMEM((keys_n + qlen, 2 * HD), jnp.bfloat16),
            ],
        ),
        out_shape=jax.ShapeDtypeStruct((tp, tokens, width), jnp.bfloat16),
        compiler_params=VMEM,
        cost_estimate=pl.CostEstimate(
            flops=4 * group * qlen * (keys_n + qlen) * HD,
            bytes_accessed=2 * keys_n * HD * 2,
            transcendentals=group * qlen * (keys_n + qlen),
        ),
        name="attend",
    )(me, *parts_q, received, received)


def solution(mesh):
    parts, tp = mesh.shape["cache"], mesh.shape["tp"]

    def local(query, qkeys, qvalues, cache_keys, cache_values, lists):
        at_cache = lax.axis_index("cache").reshape(1).astype(jnp.int32)
        at_tp = lax.axis_index("tp").reshape(1).astype(jnp.int32)
        owned = cache_keys.shape[0]
        group = query.shape[2] // qkeys.shape[2]

        banded = lax.all_to_all(
            cut_bands(cache_keys, cache_values, parts), "cache", split_axis=0, concat_axis=0, tiled=True
        )
        seen = gather_lists(lists, parts)
        cuts = cut_heads(query[0], qkeys[0], qvalues[0], at_tp, tp)
        parts_q = [cuts[0]] + [
            lax.ppermute(cuts[k], "tp", [(d, (d + k) % tp) for d in range(tp)]) for k in range(1, tp)
        ]
        picked = pick_rows(banded.reshape(parts * owned, ROWS, HD), seen, at_cache)
        received = lax.all_to_all(picked, "cache", split_axis=0, concat_axis=0, tiled=True)
        result = attend(parts_q, received, at_tp, group)
        back = lax.all_to_all(result, "tp", split_axis=0, concat_axis=0, tiled=True)
        tokens = back.shape[1]
        return back.transpose(1, 0, 2).reshape(1, tokens, tp * group * HD)

    return jax.shard_map(
        local,
        mesh=mesh,
        in_specs=(
            P("cache", "tp", None),
            P("cache", "tp", None),
            P("cache", "tp", None),
            P("cache", None, "tp"),
            P("cache", None, "tp"),
            P("cache", None),
        ),
        out_specs=P("cache", "tp", None),
        check_vma=False,
    )
```

```python
import functools

import jax
import jax.numpy as jnp
from jax import lax
from jax.experimental import pallas as pl
from jax.experimental.pallas import tpu as pltpu
from jax.sharding import PartitionSpec as P

HD = 128
EXTRA = 8
ROWS = 16
LOG2E = 1.4426950408889634
VMEM = pltpu.CompilerParams(vmem_limit_bytes=48 * 1024 * 1024)


def whole(shape):
    return pl.BlockSpec(shape, lambda *_: (0,) * len(shape))


def cut_bands(cache_keys, cache_values, parts):
    owned, plen, width = cache_keys.shape
    half = parts // 2
    rows = owned * ROWS

    def kernel(k_ref, v_ref, out_ref):
        for i in range(owned):
            at = slice(i * ROWS, (i + 1) * ROWS)
            out_ref[:half, at] = k_ref[i].reshape(half, ROWS, width)
            out_ref[half:, at] = v_ref[i].reshape(half, ROWS, width)

    return pl.pallas_call(
        kernel,
        grid=(1,),
        in_specs=[whole(cache_keys.shape), whole(cache_values.shape)],
        out_specs=whole((parts, rows, width)),
        out_shape=jax.ShapeDtypeStruct((parts, rows + EXTRA, width), cache_keys.dtype),
        compiler_params=VMEM,
        name="cut_bands",
    )(cache_keys, cache_values)


def pick_rows(bands, lists, owned):
    parts, top = lists.shape
    width = bands.shape[2]
    steps = 4
    share = parts // steps

    def kernel(lists_ref, bands_ref, out_ref):
        first = pl.program_id(0) * share

        def one(d, carry):
            for j in range(top):
                passage = lists_ref[first + d, j]
                at = pl.multiple_of(lax.rem(passage, owned) * ROWS, ROWS)
                out_ref[d, j] = bands_ref[lax.div(passage, owned), pl.ds(at, ROWS)]
            return carry

        lax.fori_loop(0, share, one, 0, unroll=2)

    return pl.pallas_call(
        kernel,
        grid_spec=pltpu.PrefetchScalarGridSpec(
            num_scalar_prefetch=1,
            grid=(steps,),
            in_specs=[whole((parts, owned * ROWS, width))],
            out_specs=pl.BlockSpec((share, top, ROWS, width), lambda s, *_: (s, 0, 0, 0)),
        ),
        out_shape=jax.ShapeDtypeStruct((parts, top, ROWS, width), bands.dtype),
        compiler_params=VMEM,
        name="pick_rows",
    )(lists, bands)


def cut_heads(query, qkeys, qvalues, me, tp):
    tokens, width = query.shape[0], query.shape[1] // tp
    small = qkeys.shape[1] // tp

    def kernel(me_ref, q_ref, k_ref, v_ref, *outs):
        for k in range(tp):
            to = lax.rem(me_ref[0] + k, tp)
            big = pl.ds(pl.multiple_of(to * width, width), width)
            own = pl.ds(pl.multiple_of(to * small, small), small)
            outs[k][:, :width] = q_ref[:, big]
            outs[k][:, width : width + small] = k_ref[:, own]
            outs[k][:, width + small :] = v_ref[:, own]

    total = width + 2 * small
    return pl.pallas_call(
        kernel,
        grid_spec=pltpu.PrefetchScalarGridSpec(
            num_scalar_prefetch=1,
            grid=(1,),
            in_specs=[whole(query.shape), whole(qkeys.shape), whole(qvalues.shape)],
            out_specs=[whole((tokens, total))] * tp,
        ),
        out_shape=[jax.ShapeDtypeStruct((tokens, total), query.dtype)] * tp,
        compiler_params=VMEM,
        name="cut_heads",
    )(me, query, qkeys, qvalues)


def attend(parts_q, received, me, group):
    tp = len(parts_q)
    tokens, total = parts_q[0].shape
    qlen = tp * tokens
    width = group * HD
    bands, top, rows, _ = received.shape
    half = bands // 2
    keys_n = half * top * rows
    per = 2
    chunk = 512
    factor = HD ** (-0.5) * LOG2E

    def kernel(me_ref, *refs):
        q_refs = refs[:tp]
        k_ref, v_ref, out_ref, scores, weights, values = refs[tp:]
        mine = me_ref[0]

        @pl.when(pl.program_id(0) == 0)
        def _():
            values[:, HD:] = jnp.ones((keys_n + qlen, HD), values.dtype)
            values[:keys_n, :HD] = v_ref[...].reshape(keys_n, HD)
            for k in range(tp):
                values[keys_n + k * tokens : keys_n + (k + 1) * tokens, :HD] = q_refs[k][:, width + HD :]

        def position(axis):
            index = lax.broadcasted_iota(jnp.int32, (qlen, qlen), axis)
            owner = lax.bitwise_and(mine - index // tokens + tp, tp - 1)
            return owner * tokens + lax.rem(index, tokens)

        sees = position(0) >= position(1)
        own_keys = jnp.concatenate([q_refs[k][:, width : width + HD] for k in range(tp)], axis=0)
        dims = (((1,), (1,)), ((), ()))
        for p in range(per):
            at = pl.ds(pl.multiple_of((pl.program_id(0) * per + p) * HD, HD), HD)
            q = jnp.concatenate([q_refs[k][:, at] for k in range(tp)], axis=0)
            s = lax.dot_general(q, own_keys, dims, preferred_element_type=jnp.float32)
            s = jnp.where(sees, s, -jnp.inf)
            scores[p, :, keys_n:] = s
            most = functools.reduce(jnp.maximum, [s[:, i : i + HD] for i in range(0, qlen, HD)])
            for c in range(0, keys_n, chunk):
                keys = k_ref[c // (top * rows) : (c + chunk) // (top * rows)].reshape(chunk, HD)
                s = lax.dot_general(q, keys, dims, preferred_element_type=jnp.float32)
                scores[p, :, c : c + chunk] = s
                most = functools.reduce(jnp.maximum, [s[:, i : i + HD] for i in range(0, chunk, HD)], most)
            m = jnp.max(most, axis=1, keepdims=True)
            for c in range(0, keys_n + qlen, 256):
                s = scores[p, :, c : c + 256]
                weights[p, :, c : c + 256] = jnp.exp2((s - m) * factor).astype(weights.dtype)
            o = jnp.dot(weights[p], values[...], preferred_element_type=jnp.float32)
            o = (o[:, :HD] / o[:, HD:]).astype(out_ref.dtype)
            for k in range(tp):
                owner = lax.bitwise_and(mine - k + tp, tp - 1)
                out_ref[owner, :, p * HD : (p + 1) * HD] = o[k * tokens : (k + 1) * tokens]

    return pl.pallas_call(
        kernel,
        grid_spec=pltpu.PrefetchScalarGridSpec(
            num_scalar_prefetch=1,
            grid=(group // per,),
            in_specs=[whole((tokens, total))] * tp
            + [
                pl.BlockSpec((half, top, rows, HD), lambda s, *_: (0, 0, 0, 0)),
                pl.BlockSpec((half, top, rows, HD), lambda s, *_: (1, 0, 0, 0)),
            ],
            out_specs=pl.BlockSpec((tp, tokens, per * HD), lambda s, *_: (0, 0, s)),
            scratch_shapes=[
                pltpu.VMEM((per, qlen, keys_n + qlen), jnp.float32),
                pltpu.VMEM((per, qlen, keys_n + qlen), jnp.bfloat16),
                pltpu.VMEM((keys_n + qlen, 2 * HD), jnp.bfloat16),
            ],
        ),
        out_shape=jax.ShapeDtypeStruct((tp, tokens, width), jnp.bfloat16),
        compiler_params=VMEM,
        cost_estimate=pl.CostEstimate(
            flops=4 * group * qlen * (keys_n + qlen) * HD,
            bytes_accessed=2 * keys_n * HD * 2,
            transcendentals=group * qlen * (keys_n + qlen),
        ),
        name="attend",
    )(me, *parts_q, received, received)


def solution(mesh):
    parts, tp = mesh.shape["cache"], mesh.shape["tp"]

    def local(query, qkeys, qvalues, cache_keys, cache_values, lists):
        at_tp = lax.axis_index("tp").reshape(1).astype(jnp.int32)
        owned = cache_keys.shape[0]
        group = query.shape[2] // qkeys.shape[2]

        bands = cut_bands(cache_keys, cache_values, parts)
        top = lists.shape[1]
        note = jnp.pad(lists.astype(bands.dtype), ((0, EXTRA - 1), (0, bands.shape[2] - top)))
        bands = bands.at[:, owned * ROWS :].set(note[None])
        bands = lax.all_to_all(bands, "cache", split_axis=0, concat_axis=0, tiled=True)
        seen = bands[:, owned * ROWS, :top].astype(jnp.int32)
        cuts = cut_heads(query[0], qkeys[0], qvalues[0], at_tp, tp)
        parts_q = [cuts[0]] + [
            lax.ppermute(cuts[k], "tp", [(d, (d + k) % tp) for d in range(tp)]) for k in range(1, tp)
        ]
        picked = pick_rows(bands, seen, owned)
        received = lax.all_to_all(picked, "cache", split_axis=0, concat_axis=0, tiled=True)
        result = attend(parts_q, received, at_tp, group)
        back = lax.all_to_all(result, "tp", split_axis=0, concat_axis=0, tiled=True)
        tokens = back.shape[1]
        return back.transpose(1, 0, 2).reshape(1, tokens, tp * group * HD)

    return jax.shard_map(
        local,
        mesh=mesh,
        in_specs=(
            P("cache", "tp", None),
            P("cache", "tp", None),
            P("cache", "tp", None),
            P("cache", None, "tp"),
            P("cache", None, "tp"),
            P("cache", None),
        ),
        out_specs=P("cache", "tp", None),
        check_vma=False,
    )
```

```python
import functools

import jax
import jax.numpy as jnp
from jax import lax
from jax.experimental import pallas as pl
from jax.experimental.pallas import tpu as pltpu
from jax.sharding import PartitionSpec as P

HD = 128
EXTRA = 8
ROWS = 16
LOG2E = 1.4426950408889634
VMEM = pltpu.CompilerParams(vmem_limit_bytes=48 * 1024 * 1024)


def whole(shape):
    return pl.BlockSpec(shape, lambda *_: (0,) * len(shape))


def cut_bands(cache_keys, cache_values, parts):
    owned, plen, width = cache_keys.shape
    half = parts // 2
    rows = owned * ROWS

    def kernel(k_ref, v_ref, out_ref, sems):
        copies = []
        for i in range(owned):
            at = pl.ds(i * ROWS, ROWS)
            copies.append(pltpu.make_async_copy(k_ref.at[i], out_ref.at[pl.ds(0, half), at], sems.at[0, i]))
            copies.append(pltpu.make_async_copy(v_ref.at[i], out_ref.at[pl.ds(half, half), at], sems.at[1, i]))
        for copy in copies:
            copy.start()
        for copy in copies:
            copy.wait()

    return pl.pallas_call(
        kernel,
        in_specs=[pl.BlockSpec(memory_space=pl.ANY)] * 2,
        out_specs=pl.BlockSpec(memory_space=pltpu.VMEM),
        scratch_shapes=[pltpu.SemaphoreType.DMA((2, owned))],
        out_shape=jax.ShapeDtypeStruct((parts, rows + EXTRA, width), cache_keys.dtype),
        name="cut_bands",
    )(
        cache_keys.reshape(owned, half, ROWS, width),
        cache_values.reshape(owned, half, ROWS, width),
    )


def pick_rows(bands, lists, owned):
    parts, top = lists.shape
    width = bands.shape[2]
    assert owned & (owned - 1) == 0
    shift = owned.bit_length() - 1

    def kernel(lists_ref, bands_ref, out_ref):
        def one(d, carry):
            for j in range(top):
                passage = lists_ref[d, j]
                at = pl.multiple_of(lax.bitwise_and(passage, owned - 1) * ROWS, ROWS)
                out_ref[d, j] = bands_ref[lax.shift_right_logical(passage, shift), pl.ds(at, ROWS)]
            return carry

        lax.fori_loop(0, parts, one, 0, unroll=4)

    return pl.pallas_call(
        kernel,
        in_specs=[pl.BlockSpec(memory_space=pltpu.SMEM), pl.BlockSpec(memory_space=pltpu.VMEM)],
        out_specs=pl.BlockSpec(memory_space=pltpu.VMEM),
        out_shape=jax.ShapeDtypeStruct((parts, top, ROWS, width), bands.dtype),
        compiler_params=VMEM,
        name="pick_rows",
    )(lists, bands)


def cut_heads(query, qkeys, qvalues, me, tp):
    tokens, width = query.shape[0], query.shape[1] // tp
    small = qkeys.shape[1] // tp

    def kernel(me_ref, q_ref, k_ref, v_ref, *outs):
        for k in range(tp):
            to = lax.rem(me_ref[0] + k, tp)
            big = pl.ds(pl.multiple_of(to * width, width), width)
            own = pl.ds(pl.multiple_of(to * small, small), small)
            outs[k][:, :width] = q_ref[:, big]
            outs[k][:, width : width + small] = k_ref[:, own]
            outs[k][:, width + small :] = v_ref[:, own]

    total = width + 2 * small
    return pl.pallas_call(
        kernel,
        grid_spec=pltpu.PrefetchScalarGridSpec(
            num_scalar_prefetch=1,
            grid=(1,),
            in_specs=[whole(query.shape), whole(qkeys.shape), whole(qvalues.shape)],
            out_specs=[whole((tokens, total))] * tp,
        ),
        out_shape=[jax.ShapeDtypeStruct((tokens, total), query.dtype)] * tp,
        compiler_params=VMEM,
        name="cut_heads",
    )(me, query, qkeys, qvalues)


def attend(parts_q, received, me, group):
    tp = len(parts_q)
    tokens, total = parts_q[0].shape
    qlen = tp * tokens
    width = group * HD
    bands, top, rows, _ = received.shape
    half = bands // 2
    keys_n = half * top * rows
    all_n = keys_n + qlen
    per = 2
    chunk = 512
    span = 1024
    factor = HD ** (-0.5) * LOG2E
    dims = (((1,), (1,)), ((), ()))

    def lane_max(s, most):
        pieces = [s[:, i : i + HD] for i in range(0, s.shape[1], HD)]
        return functools.reduce(jnp.maximum, pieces if most is None else [most] + pieces)

    def kernel(me_ref, *refs):
        q_refs = refs[:tp]
        k_ref, v_ref, out_ref, scores, values = refs[tp:]
        mine = me_ref[0]
        values[:, HD:] = jnp.ones((all_n, HD), values.dtype)
        values[:keys_n, :HD] = v_ref[...].reshape(keys_n, HD)
        for k in range(tp):
            values[keys_n + k * tokens : keys_n + (k + 1) * tokens, :HD] = q_refs[k][:, width + HD :]

        def position(axis):
            index = lax.broadcasted_iota(jnp.int32, (qlen, qlen), axis)
            owner = lax.bitwise_and(mine - index // tokens + tp, tp - 1)
            return owner * tokens + lax.rem(index, tokens)

        sees = jnp.concatenate([position(0) >= position(1)] * per, axis=0)
        own_keys = jnp.concatenate([q_refs[k][:, width : width + HD] for k in range(tp)], axis=0)

        def score_steps(g):
            heads = [slice((g * per + p) * HD, (g * per + p + 1) * HD) for p in range(per)]
            q = jnp.concatenate([q_refs[k][:, at] for at in heads for k in range(tp)], axis=0)

            def own_step(most):
                s = lax.dot_general(q, own_keys, dims, preferred_element_type=jnp.float32)
                s = jnp.where(sees, s, -jnp.inf)
                scores[g % 2, :, keys_n:] = s
                return lane_max(s, most)

            def step(c, most):
                keys = k_ref[c // (top * rows) : (c + chunk) // (top * rows)].reshape(chunk, HD)
                s = lax.dot_general(q, keys, dims, preferred_element_type=jnp.float32)
                scores[g % 2, :, c : c + chunk] = s
                return lane_max(s, most)

            return [own_step] + [functools.partial(step, c) for c in range(0, keys_n, chunk)]

        most = None
        for step in score_steps(0):
            most = step(most)
        spans = [(c, min(c + span, all_n)) for c in range(0, all_n, span)]
        groups = group // per
        for g in range(groups):
            m = jnp.max(most, axis=1, keepdims=True)
            steps = score_steps(g + 1) if g + 1 < groups else []
            most, total_o, done = None, None, 0
            for i, (lo, hi) in enumerate(spans):
                upto = -(-len(steps) * (i + 1) // len(spans))
                for step in steps[done:upto]:
                    most = step(most)
                done = upto
                w = jnp.exp2((scores[g % 2, :, lo:hi] - m) * factor).astype(values.dtype)
                o = jnp.dot(w, values[lo:hi], preferred_element_type=jnp.float32)
                total_o = o if total_o is None else total_o + o
            o = (total_o[:, :HD] / total_o[:, HD:]).astype(out_ref.dtype)
            for p in range(per):
                for k in range(tp):
                    owner = lax.bitwise_and(mine - k + tp, tp - 1)
                    at = p * qlen + k * tokens
                    out_ref[owner, :, (g * per + p) * HD : (g * per + p + 1) * HD] = o[at : at + tokens]

    return pl.pallas_call(
        kernel,
        grid_spec=pltpu.PrefetchScalarGridSpec(
            num_scalar_prefetch=1,
            grid=(1,),
            in_specs=[whole((tokens, total))] * tp
            + [
                pl.BlockSpec((half, top, rows, HD), lambda s, *_: (0, 0, 0, 0)),
                pl.BlockSpec((half, top, rows, HD), lambda s, *_: (1, 0, 0, 0)),
            ],
            out_specs=whole((tp, tokens, width)),
            scratch_shapes=[
                pltpu.VMEM((2, per * qlen, all_n), jnp.float32),
                pltpu.VMEM((all_n, 2 * HD), jnp.bfloat16),
            ],
        ),
        out_shape=jax.ShapeDtypeStruct((tp, tokens, width), jnp.bfloat16),
        compiler_params=VMEM,
        cost_estimate=pl.CostEstimate(
            flops=4 * group * qlen * all_n * HD,
            bytes_accessed=2 * keys_n * HD * 2,
            transcendentals=group * qlen * all_n,
        ),
        name="attend",
    )(me, *parts_q, received, received)


def solution(mesh):
    parts, tp = mesh.shape["cache"], mesh.shape["tp"]

    def local(query, qkeys, qvalues, cache_keys, cache_values, lists):
        at_tp = lax.axis_index("tp").reshape(1).astype(jnp.int32)
        owned = cache_keys.shape[0]
        group = query.shape[2] // qkeys.shape[2]

        bands = cut_bands(cache_keys, cache_values, parts)
        top = lists.shape[1]
        note = jnp.pad(lists.astype(bands.dtype), ((0, EXTRA - 1), (0, bands.shape[2] - top)))
        bands = bands.at[:, owned * ROWS :].set(note[None])
        bands = lax.all_to_all(bands, "cache", split_axis=0, concat_axis=0, tiled=True)
        seen = bands[:, owned * ROWS, :top].astype(jnp.int32)
        cuts = cut_heads(query[0], qkeys[0], qvalues[0], at_tp, tp)
        parts_q = [cuts[0]] + [
            lax.ppermute(cuts[k], "tp", [(d, (d + k) % tp) for d in range(tp)]) for k in range(1, tp)
        ]
        picked = pick_rows(bands, seen, owned)
        received = lax.all_to_all(picked, "cache", split_axis=0, concat_axis=0, tiled=True)
        result = attend(parts_q, received, at_tp, group)
        back = lax.all_to_all(result, "tp", split_axis=0, concat_axis=0, tiled=True)
        tokens = back.shape[1]
        return back.transpose(1, 0, 2).reshape(1, tokens, tp * group * HD)

    return jax.shard_map(
        local,
        mesh=mesh,
        in_specs=(
            P("cache", "tp", None),
            P("cache", "tp", None),
            P("cache", "tp", None),
            P("cache", None, "tp"),
            P("cache", None, "tp"),
            P("cache", None),
        ),
        out_specs=P("cache", "tp", None),
        check_vma=False,
    )
```

```python
import functools

import jax
import jax.numpy as jnp
from jax import lax
from jax.experimental import pallas as pl
from jax.experimental.pallas import tpu as pltpu
from jax.sharding import PartitionSpec as P

HD = 128
EXTRA = 8
ROWS = 16
LOG2E = 1.4426950408889634
VMEM = pltpu.CompilerParams(vmem_limit_bytes=48 * 1024 * 1024)


def whole(shape):
    return pl.BlockSpec(shape, lambda *_: (0,) * len(shape))


def cut_bands(cache_keys, cache_values, lists, parts):
    owned, plen, width = cache_keys.shape
    half = parts // 2
    rows = owned * ROWS
    top = lists.shape[1]

    def kernel(lists_ref, k_ref, v_ref, out_ref, note_ref):
        for i in range(owned):
            at = slice(i * ROWS, (i + 1) * ROWS)
            out_ref[:half, at] = k_ref[i].reshape(half, ROWS, width)
            out_ref[half:, at] = v_ref[i].reshape(half, ROWS, width)
        lane = lax.broadcasted_iota(jnp.int32, (EXTRA, width), 1)
        note = jnp.zeros((EXTRA, width), jnp.int32)
        for j in range(top):
            note = jnp.where(lane == j, lists_ref[0, j], note)
        note_ref[...] = note.astype(jnp.float32).astype(note_ref.dtype)

    return pl.pallas_call(
        kernel,
        grid=(1,),
        in_specs=[
            pl.BlockSpec(memory_space=pltpu.SMEM),
            whole(cache_keys.shape),
            whole(cache_values.shape),
        ],
        out_specs=[whole((parts, rows, width)), whole((EXTRA, width))],
        out_shape=[
            jax.ShapeDtypeStruct((parts, rows + EXTRA, width), cache_keys.dtype),
            jax.ShapeDtypeStruct((EXTRA, width), cache_keys.dtype),
        ],
        compiler_params=VMEM,
        name="cut_bands",
    )(lists, cache_keys, cache_values)


def pick_rows(bands, lists, owned):
    parts, top = lists.shape
    width = bands.shape[2]
    assert owned & (owned - 1) == 0
    shift = owned.bit_length() - 1

    def kernel(lists_ref, bands_ref, out_ref):
        def one(d, carry):
            found = []
            for j in range(2 * top):
                passage = lists_ref[2 * d + j // top, j % top]
                at = pl.multiple_of(lax.bitwise_and(passage, owned - 1) * ROWS, ROWS)
                found.append(bands_ref[lax.shift_right_logical(passage, shift), pl.ds(at, ROWS)])
            for j in range(2 * top):
                out_ref[2 * d + j // top, j % top] = found[j]
            return carry

        lax.fori_loop(0, parts // 2, one, 0, unroll=2)

    return pl.pallas_call(
        kernel,
        in_specs=[pl.BlockSpec(memory_space=pltpu.SMEM), pl.BlockSpec(memory_space=pltpu.VMEM)],
        out_specs=pl.BlockSpec(memory_space=pltpu.VMEM),
        out_shape=jax.ShapeDtypeStruct((parts, top, ROWS, width), bands.dtype),
        compiler_params=VMEM,
        name="pick_rows",
    )(lists, bands)


def cut_heads(query, qkeys, qvalues, me, tp):
    tokens, width = query.shape[0], query.shape[1] // tp
    small = qkeys.shape[1] // tp

    def kernel(me_ref, q_ref, k_ref, v_ref, *outs):
        for k in range(tp):
            to = lax.rem(me_ref[0] + k, tp)
            big = pl.ds(pl.multiple_of(to * width, width), width)
            own = pl.ds(pl.multiple_of(to * small, small), small)
            outs[k][:, :width] = q_ref[:, big]
            outs[k][:, width : width + small] = k_ref[:, own]
            outs[k][:, width + small :] = v_ref[:, own]

    total = width + 2 * small
    return pl.pallas_call(
        kernel,
        grid_spec=pltpu.PrefetchScalarGridSpec(
            num_scalar_prefetch=1,
            grid=(1,),
            in_specs=[whole(query.shape), whole(qkeys.shape), whole(qvalues.shape)],
            out_specs=[whole((tokens, total))] * tp,
        ),
        out_shape=[jax.ShapeDtypeStruct((tokens, total), query.dtype)] * tp,
        compiler_params=VMEM,
        name="cut_heads",
    )(me, query, qkeys, qvalues)


def attend(parts_q, received, me, group):
    tp = len(parts_q)
    tokens, total = parts_q[0].shape
    qlen = tp * tokens
    width = group * HD
    bands, top, rows, _ = received.shape
    half = bands // 2
    keys_n = half * top * rows
    all_n = keys_n + qlen
    per = 2
    chunk = 512
    span = 1024
    factor = HD ** (-0.5) * LOG2E
    dims = (((1,), (1,)), ((), ()))

    def lane_max(s, most):
        pieces = [s[:, i : i + HD] for i in range(0, s.shape[1], HD)]
        return functools.reduce(jnp.maximum, pieces if most is None else [most] + pieces)

    def kernel(me_ref, *refs):
        q_refs = refs[:tp]
        k_ref, v_ref, out_ref, scores, values = refs[tp:]
        mine = me_ref[0]
        values[:, HD:] = jnp.ones((all_n, HD), values.dtype)
        values[:keys_n, :HD] = v_ref[...].reshape(keys_n, HD)
        for k in range(tp):
            values[keys_n + k * tokens : keys_n + (k + 1) * tokens, :HD] = q_refs[k][:, width + HD :]

        def position(axis):
            index = lax.broadcasted_iota(jnp.int32, (qlen, qlen), axis)
            owner = lax.bitwise_and(mine - index // tokens + tp, tp - 1)
            return owner * tokens + lax.rem(index, tokens)

        sees = jnp.concatenate([position(0) >= position(1)] * per, axis=0)
        own_keys = jnp.concatenate([q_refs[k][:, width : width + HD] for k in range(tp)], axis=0)

        def score_steps(g):
            heads = [slice((g * per + p) * HD, (g * per + p + 1) * HD) for p in range(per)]
            q = jnp.concatenate([q_refs[k][:, at] for at in heads for k in range(tp)], axis=0)

            def own_step(most):
                s = lax.dot_general(q, own_keys, dims, preferred_element_type=jnp.float32)
                s = jnp.where(sees, s, -jnp.inf)
                scores[g % 2, :, keys_n:] = s
                return lane_max(s, most)

            def step(c, most):
                keys = k_ref[c // (top * rows) : (c + chunk) // (top * rows)].reshape(chunk, HD)
                s = lax.dot_general(q, keys, dims, preferred_element_type=jnp.float32)
                scores[g % 2, :, c : c + chunk] = s
                return lane_max(s, most)

            return [own_step] + [functools.partial(step, c) for c in range(0, keys_n, chunk)]

        most = None
        for step in score_steps(0):
            most = step(most)
        spans = [(c, min(c + span, all_n)) for c in range(0, all_n, span)]
        groups = group // per
        for g in range(groups):
            m = jnp.max(most, axis=1, keepdims=True)
            steps = score_steps(g + 1) if g + 1 < groups else []
            most, total_o, done = None, None, 0
            for i, (lo, hi) in enumerate(spans):
                upto = -(-len(steps) * (i + 1) // len(spans))
                for step in steps[done:upto]:
                    most = step(most)
                done = upto
                w = jnp.exp2((scores[g % 2, :, lo:hi] - m) * factor).astype(values.dtype)
                o = jnp.dot(w, values[lo:hi], preferred_element_type=jnp.float32)
                total_o = o if total_o is None else total_o + o
            o = (total_o[:, :HD] / total_o[:, HD:]).astype(out_ref.dtype)
            for p in range(per):
                for k in range(tp):
                    owner = lax.bitwise_and(mine - k + tp, tp - 1)
                    at = p * qlen + k * tokens
                    out_ref[owner, :, (g * per + p) * HD : (g * per + p + 1) * HD] = o[at : at + tokens]

    return pl.pallas_call(
        kernel,
        grid_spec=pltpu.PrefetchScalarGridSpec(
            num_scalar_prefetch=1,
            grid=(1,),
            in_specs=[whole((tokens, total))] * tp
            + [
                pl.BlockSpec((half, top, rows, HD), lambda s, *_: (0, 0, 0, 0)),
                pl.BlockSpec((half, top, rows, HD), lambda s, *_: (1, 0, 0, 0)),
            ],
            out_specs=whole((tp, tokens, width)),
            scratch_shapes=[
                pltpu.VMEM((2, per * qlen, all_n), jnp.float32),
                pltpu.VMEM((all_n, 2 * HD), jnp.bfloat16),
            ],
        ),
        out_shape=jax.ShapeDtypeStruct((tp, tokens, width), jnp.bfloat16),
        compiler_params=VMEM,
        cost_estimate=pl.CostEstimate(
            flops=4 * group * qlen * all_n * HD,
            bytes_accessed=2 * keys_n * HD * 2,
            transcendentals=group * qlen * all_n,
        ),
        name="attend",
    )(me, *parts_q, received, received)


def join_heads(back):
    groups, tokens, width = back.shape

    def kernel(in_ref, out_ref, sems):
        copies = [
            pltpu.make_async_copy(in_ref.at[g], out_ref.at[0, :, pl.ds(g * width, width)], sems.at[g])
            for g in range(groups)
        ]
        for copy in copies:
            copy.start()
        for copy in copies:
            copy.wait()

    return pl.pallas_call(
        kernel,
        in_specs=[pl.BlockSpec(memory_space=pltpu.VMEM)],
        out_specs=pl.BlockSpec(memory_space=pl.ANY),
        scratch_shapes=[pltpu.SemaphoreType.DMA((groups,))],
        out_shape=jax.ShapeDtypeStruct((1, tokens, groups * width), back.dtype),
        compiler_params=VMEM,
        name="join_heads",
    )(back)


def solution(mesh):
    parts, tp = mesh.shape["cache"], mesh.shape["tp"]

    def local(query, qkeys, qvalues, cache_keys, cache_values, lists):
        at_tp = lax.axis_index("tp").reshape(1).astype(jnp.int32)
        owned = cache_keys.shape[0]
        group = query.shape[2] // qkeys.shape[2]

        top = lists.shape[1]
        bands, note = cut_bands(cache_keys, cache_values, lists, parts)
        bands = bands.at[:, owned * ROWS :].set(note[None])
        bands = lax.all_to_all(bands, "cache", split_axis=0, concat_axis=0, tiled=True)
        seen = bands[:, owned * ROWS, :top].astype(jnp.int32)
        cuts = cut_heads(query[0], qkeys[0], qvalues[0], at_tp, tp)
        parts_q = [cuts[0]] + [
            lax.ppermute(cuts[k], "tp", [(d, (d + k) % tp) for d in range(tp)]) for k in range(1, tp)
        ]
        picked = pick_rows(bands, seen, owned)
        received = lax.all_to_all(picked, "cache", split_axis=0, concat_axis=0, tiled=True)
        result = attend(parts_q, received, at_tp, group)
        back = lax.all_to_all(result, "tp", split_axis=0, concat_axis=0, tiled=True)
        return join_heads(back)

    return jax.shard_map(
        local,
        mesh=mesh,
        in_specs=(
            P("cache", "tp", None),
            P("cache", "tp", None),
            P("cache", "tp", None),
            P("cache", None, "tp"),
            P("cache", None, "tp"),
            P("cache", None),
        ),
        out_specs=P("cache", "tp", None),
        check_vma=False,
    )
```

```python
import functools

import jax
import jax.numpy as jnp
from jax import lax
from jax.experimental import pallas as pl
from jax.experimental.pallas import tpu as pltpu
from jax.sharding import PartitionSpec as P

HD = 128
EXTRA = 8
ROWS = 16
LOG2E = 1.4426950408889634
LIMIT = 62 * 1024 * 1024 + 512 * 1024
VMEM = pltpu.CompilerParams(vmem_limit_bytes=48 * 1024 * 1024)


def whole(shape):
    return pl.BlockSpec(shape, lambda *_: (0,) * len(shape))


def cut_bands(cache_keys, cache_values, lists, parts):
    owned, plen, width = cache_keys.shape
    half = parts // 2
    rows = owned * ROWS
    top = lists.shape[1]
    pieces = 2
    part = plen // pieces

    def kernel(lists_ref, k_ref, v_ref, out_ref, list_buf, bufs, list_sem, sems):
        list_copy = pltpu.make_async_copy(lists_ref, list_buf, list_sem)
        list_copy.start()
        copies = {}
        for i in range(owned):
            for side, ref in enumerate((k_ref, v_ref)):
                for n in range(pieces):
                    at = pl.ds(n * part, part)
                    copy = pltpu.make_async_copy(ref.at[i, at], bufs.at[side, i, at], sems.at[side, i, n])
                    copy.start()
                    copies[side, i, n] = copy
        list_copy.wait()
        spread = lax.broadcasted_iota(jnp.int32, (top, width), 0) == lax.broadcasted_iota(jnp.int32, (top, width), 1)
        note = jnp.dot(
            list_buf[...].astype(jnp.bfloat16), spread.astype(jnp.bfloat16), preferred_element_type=jnp.float32
        )
        out_ref[:, rows:] = jnp.broadcast_to(note.astype(out_ref.dtype)[None], (parts, EXTRA, width))
        for i in range(owned):
            at = slice(i * ROWS, (i + 1) * ROWS)
            for side in range(2):
                for n in range(pieces):
                    copies[side, i, n].wait()
                out_ref[side * half : (side + 1) * half, at] = bufs[side, i].reshape(half, ROWS, width)

    return pl.pallas_call(
        kernel,
        in_specs=[pl.BlockSpec(memory_space=pl.ANY)] * 3,
        out_specs=pl.BlockSpec(memory_space=pltpu.VMEM),
        scratch_shapes=[
            pltpu.VMEM(lists.shape, lists.dtype),
            pltpu.VMEM((2, owned, plen, width), cache_keys.dtype),
            pltpu.SemaphoreType.DMA,
            pltpu.SemaphoreType.DMA((2, owned, pieces)),
        ],
        out_shape=jax.ShapeDtypeStruct((parts, rows + EXTRA, width), cache_keys.dtype),
        compiler_params=pltpu.CompilerParams(vmem_limit_bytes=LIMIT),
        name="cut_bands",
    )(lists, cache_keys, cache_values)


def pick_rows(bands, lists, owned):
    parts, top = lists.shape
    width = bands.shape[2]
    assert owned & (owned - 1) == 0
    shift = owned.bit_length() - 1

    steps = 16
    share = parts // steps

    def kernel(lists_ref, bands_ref, out_ref, buf, sems):
        def one(d, carry):
            found = []
            for j in range(top):
                passage = lists_ref[d, j]
                at = pl.multiple_of(lax.bitwise_and(passage, owned - 1) * ROWS, ROWS)
                found.append(bands_ref[lax.shift_right_logical(passage, shift), pl.ds(at, ROWS)])
            for j in range(top):
                buf[d, j] = found[j]
            return carry

        copies = []
        for step in range(steps):
            lax.fori_loop(step * share, (step + 1) * share, one, 0, unroll=4)
            at = pl.ds(step * share, share)
            copies.append(pltpu.make_async_copy(buf.at[at], out_ref.at[at], sems.at[step]))
            copies[-1].start()
        for copy in copies:
            copy.wait()

    return pl.pallas_call(
        kernel,
        in_specs=[pl.BlockSpec(memory_space=pltpu.SMEM), pl.BlockSpec(memory_space=pltpu.VMEM)],
        out_specs=pl.BlockSpec(memory_space=pl.ANY),
        scratch_shapes=[
            pltpu.VMEM((parts, top, ROWS, width), bands.dtype),
            pltpu.SemaphoreType.DMA((steps,)),
        ],
        out_shape=jax.ShapeDtypeStruct((parts, top, ROWS, width), bands.dtype),
        compiler_params=VMEM,
        name="pick_rows",
    )(lists, bands)


def cut_heads(query, qkeys, qvalues, me, tp):
    tokens, width = query.shape[0], query.shape[1] // tp
    small = qkeys.shape[1] // tp

    def kernel(me_ref, q_ref, k_ref, v_ref, *outs):
        for k in range(tp):
            to = lax.rem(me_ref[0] + k, tp)
            big = pl.ds(pl.multiple_of(to * width, width), width)
            own = pl.ds(pl.multiple_of(to * small, small), small)
            outs[k][:, :width] = q_ref[:, big]
            outs[k][:, width : width + small] = k_ref[:, own]
            outs[k][:, width + small :] = v_ref[:, own]

    total = width + 2 * small
    return pl.pallas_call(
        kernel,
        grid_spec=pltpu.PrefetchScalarGridSpec(
            num_scalar_prefetch=1,
            grid=(1,),
            in_specs=[whole(query.shape), whole(qkeys.shape), whole(qvalues.shape)],
            out_specs=[whole((tokens, total))] * tp,
        ),
        out_shape=[jax.ShapeDtypeStruct((tokens, total), query.dtype)] * tp,
        compiler_params=VMEM,
        name="cut_heads",
    )(me, query, qkeys, qvalues)


def attend(parts_q, received, me, group):
    tp = len(parts_q)
    tokens, total = parts_q[0].shape
    qlen = tp * tokens
    width = group * HD
    bands, top, rows, _ = received.shape
    half = bands // 2
    keys_n = half * top * rows
    all_n = keys_n + qlen
    per = 2
    chunk = 512
    span = 1024
    factor = HD ** (-0.5) * LOG2E
    dims = (((1,), (1,)), ((), ()))

    def lane_max(s, most):
        pieces = [s[:, i : i + HD] for i in range(0, s.shape[1], HD)]
        return functools.reduce(jnp.maximum, pieces if most is None else [most] + pieces)

    def kernel(me_ref, *refs):
        q_refs = refs[:tp]
        k_ref, v_ref, out_ref, scores, values = refs[tp:]
        mine = me_ref[0]
        values[:, HD:] = jnp.ones((all_n, HD), values.dtype)
        values[:keys_n, :HD] = v_ref[...].reshape(keys_n, HD)
        for k in range(tp):
            values[keys_n + k * tokens : keys_n + (k + 1) * tokens, :HD] = q_refs[k][:, width + HD :]

        def position(axis):
            index = lax.broadcasted_iota(jnp.int32, (qlen, qlen), axis)
            owner = lax.bitwise_and(mine - index // tokens + tp, tp - 1)
            return owner * tokens + lax.rem(index, tokens)

        sees = jnp.concatenate([position(0) >= position(1)] * per, axis=0)
        own_keys = jnp.concatenate([q_refs[k][:, width : width + HD] for k in range(tp)], axis=0)

        def score_steps(g):
            heads = [slice((g * per + p) * HD, (g * per + p + 1) * HD) for p in range(per)]
            q = jnp.concatenate([q_refs[k][:, at] for at in heads for k in range(tp)], axis=0)

            def own_step(most):
                s = lax.dot_general(q, own_keys, dims, preferred_element_type=jnp.float32)
                s = jnp.where(sees, s, -jnp.inf)
                scores[g % 2, :, keys_n:] = s
                return lane_max(s, most)

            def step(c, most):
                keys = k_ref[c // (top * rows) : (c + chunk) // (top * rows)].reshape(chunk, HD)
                s = lax.dot_general(q, keys, dims, preferred_element_type=jnp.float32)
                scores[g % 2, :, c : c + chunk] = s
                return lane_max(s, most)

            return [own_step] + [functools.partial(step, c) for c in range(0, keys_n, chunk)]

        most = None
        for step in score_steps(0):
            most = step(most)
        spans = [(c, min(c + span, all_n)) for c in range(0, all_n, span)]
        groups = group // per
        for g in range(groups):
            m = jnp.max(most, axis=1, keepdims=True)
            steps = score_steps(g + 1) if g + 1 < groups else []
            most, total_o, done = None, None, 0
            for i, (lo, hi) in enumerate(spans):
                upto = -(-len(steps) * (i + 1) // len(spans))
                for step in steps[done:upto]:
                    most = step(most)
                done = upto
                w = jnp.exp2((scores[g % 2, :, lo:hi] - m) * factor).astype(values.dtype)
                o = jnp.dot(w, values[lo:hi], preferred_element_type=jnp.float32)
                total_o = o if total_o is None else total_o + o
            o = (total_o[:, :HD] / total_o[:, HD:]).astype(out_ref.dtype)
            for p in range(per):
                for k in range(tp):
                    owner = lax.bitwise_and(mine - k + tp, tp - 1)
                    at = p * qlen + k * tokens
                    out_ref[owner, :, (g * per + p) * HD : (g * per + p + 1) * HD] = o[at : at + tokens]

    return pl.pallas_call(
        kernel,
        grid_spec=pltpu.PrefetchScalarGridSpec(
            num_scalar_prefetch=1,
            grid=(1,),
            in_specs=[whole((tokens, total))] * tp
            + [
                pl.BlockSpec((half, top, rows, HD), lambda s, *_: (0, 0, 0, 0)),
                pl.BlockSpec((half, top, rows, HD), lambda s, *_: (1, 0, 0, 0)),
            ],
            out_specs=whole((tp, tokens, width)),
            scratch_shapes=[
                pltpu.VMEM((2, per * qlen, all_n), jnp.float32),
                pltpu.VMEM((all_n, 2 * HD), jnp.bfloat16),
            ],
        ),
        out_shape=jax.ShapeDtypeStruct((tp, tokens, width), jnp.bfloat16),
        compiler_params=VMEM,
        cost_estimate=pl.CostEstimate(
            flops=4 * group * qlen * all_n * HD,
            bytes_accessed=2 * keys_n * HD * 2,
            transcendentals=group * qlen * all_n,
        ),
        name="attend",
    )(me, *parts_q, received, received)


def join_heads(back):
    groups, tokens, width = back.shape

    def kernel(in_ref, out_ref, sems):
        copies = [
            pltpu.make_async_copy(in_ref.at[g], out_ref.at[0, :, pl.ds(g * width, width)], sems.at[g])
            for g in range(groups)
        ]
        for copy in copies:
            copy.start()
        for copy in copies:
            copy.wait()

    return pl.pallas_call(
        kernel,
        in_specs=[pl.BlockSpec(memory_space=pltpu.VMEM)],
        out_specs=pl.BlockSpec(memory_space=pl.ANY),
        scratch_shapes=[pltpu.SemaphoreType.DMA((groups,))],
        out_shape=jax.ShapeDtypeStruct((1, tokens, groups * width), back.dtype),
        compiler_params=VMEM,
        name="join_heads",
    )(back)


def solution(mesh):
    parts, tp = mesh.shape["cache"], mesh.shape["tp"]

    def local(query, qkeys, qvalues, cache_keys, cache_values, lists):
        at_tp = lax.axis_index("tp").reshape(1).astype(jnp.int32)
        owned = cache_keys.shape[0]
        group = query.shape[2] // qkeys.shape[2]

        top = lists.shape[1]
        bands = cut_bands(cache_keys, cache_values, lists, parts)
        bands = lax.all_to_all(bands, "cache", split_axis=0, concat_axis=0, tiled=True)
        seen = bands[:, owned * ROWS, :top].astype(jnp.int32)
        cuts = cut_heads(query[0], qkeys[0], qvalues[0], at_tp, tp)
        parts_q = [cuts[0]] + [
            lax.ppermute(cuts[k], "tp", [(d, (d + k) % tp) for d in range(tp)]) for k in range(1, tp)
        ]
        picked = pick_rows(bands, seen, owned)
        received = lax.all_to_all(picked, "cache", split_axis=0, concat_axis=0, tiled=True)
        result = attend(parts_q, received, at_tp, group)
        back = lax.all_to_all(result, "tp", split_axis=0, concat_axis=0, tiled=True)
        return join_heads(back)

    return jax.shard_map(
        local,
        mesh=mesh,
        in_specs=(
            P("cache", "tp", None),
            P("cache", "tp", None),
            P("cache", "tp", None),
            P("cache", None, "tp"),
            P("cache", None, "tp"),
            P("cache", None),
        ),
        out_specs=P("cache", "tp", None),
        check_vma=False,
    )
```

```python
import functools

import jax
import jax.numpy as jnp
from jax import lax
from jax.experimental import pallas as pl
from jax.experimental.pallas import tpu as pltpu
from jax.sharding import PartitionSpec as P

HD = 128
EXTRA = 8
ROWS = 16
LOG2E = 1.4426950408889634
VMEM = pltpu.CompilerParams(vmem_limit_bytes=48 * 1024 * 1024)


def whole(shape):
    return pl.BlockSpec(shape, lambda *_: (0,) * len(shape))


def cut_bands(cache_keys, cache_values, lists, parts):
    owned, plen, width = cache_keys.shape
    half = parts // 2
    rows = owned * ROWS
    top = lists.shape[1]
    pieces = 4
    part = plen // pieces

    def kernel(lists_ref, k_ref, v_ref, out_ref, list_buf, bufs, list_sem, sems):
        list_copy = pltpu.make_async_copy(lists_ref, list_buf, list_sem)
        list_copy.start()
        copies = {}
        for i in range(owned):
            for side, ref in enumerate((k_ref, v_ref)):
                for n in range(pieces):
                    at = pl.ds(n * part, part)
                    copy = pltpu.make_async_copy(ref.at[i, at], bufs.at[side, i, at], sems.at[side, i, n])
                    copy.start()
                    copies[side, i, n] = copy
        list_copy.wait()
        spread = lax.broadcasted_iota(jnp.int32, (top, width), 0) == lax.broadcasted_iota(jnp.int32, (top, width), 1)
        note = jnp.dot(
            list_buf[...].astype(jnp.bfloat16), spread.astype(jnp.bfloat16), preferred_element_type=jnp.float32
        )
        out_ref[:, rows:] = jnp.broadcast_to(note.astype(out_ref.dtype)[None], (parts, EXTRA, width))
        for i in range(owned):
            at = slice(i * ROWS, (i + 1) * ROWS)
            for side in range(2):
                for n in range(pieces):
                    copies[side, i, n].wait()
                out_ref[side * half : (side + 1) * half, at] = bufs[side, i].reshape(half, ROWS, width)

    return pl.pallas_call(
        kernel,
        in_specs=[pl.BlockSpec(memory_space=pltpu.HBM)] * 3,
        out_specs=pl.BlockSpec(memory_space=pltpu.VMEM),
        scratch_shapes=[
            pltpu.VMEM(lists.shape, lists.dtype),
            pltpu.VMEM((2, owned, plen, width), cache_keys.dtype),
            pltpu.SemaphoreType.DMA,
            pltpu.SemaphoreType.DMA((2, owned, pieces)),
        ],
        out_shape=jax.ShapeDtypeStruct((parts, rows + EXTRA, width), cache_keys.dtype),
        compiler_params=pltpu.CompilerParams(vmem_limit_bytes=40 * 1024 * 1024),
        name="cut_bands",
    )(
        pltpu.with_memory_space_constraint(lists, pltpu.HBM),
        pltpu.with_memory_space_constraint(cache_keys, pltpu.HBM),
        pltpu.with_memory_space_constraint(cache_values, pltpu.HBM),
    )


def pick_rows(bands, lists, owned):
    parts, top = lists.shape
    width = bands.shape[2]
    assert owned & (owned - 1) == 0
    shift = owned.bit_length() - 1

    steps = 16
    share = parts // steps

    def kernel(lists_ref, bands_ref, out_ref, buf, sems):
        def one(d, carry):
            found = []
            for j in range(top):
                passage = lists_ref[d, j]
                at = pl.multiple_of(lax.bitwise_and(passage, owned - 1) * ROWS, ROWS)
                found.append(bands_ref[lax.shift_right_logical(passage, shift), pl.ds(at, ROWS)])
            for j in range(top):
                buf[d, j] = found[j]
            return carry

        copies = []
        for step in range(steps):
            lax.fori_loop(step * share, (step + 1) * share, one, 0, unroll=4)
            at = pl.ds(step * share, share)
            copies.append(pltpu.make_async_copy(buf.at[at], out_ref.at[at], sems.at[step]))
            copies[-1].start()
        for copy in copies:
            copy.wait()

    return pl.pallas_call(
        kernel,
        in_specs=[pl.BlockSpec(memory_space=pltpu.SMEM), pl.BlockSpec(memory_space=pltpu.VMEM)],
        out_specs=pl.BlockSpec(memory_space=pl.ANY),
        scratch_shapes=[
            pltpu.VMEM((parts, top, ROWS, width), bands.dtype),
            pltpu.SemaphoreType.DMA((steps,)),
        ],
        out_shape=jax.ShapeDtypeStruct((parts, top, ROWS, width), bands.dtype),
        compiler_params=VMEM,
        name="pick_rows",
    )(lists, bands)


def cut_heads(query, qkeys, qvalues, me, tp):
    tokens, width = query.shape[0], query.shape[1] // tp
    small = qkeys.shape[1] // tp

    def kernel(me_ref, q_ref, k_ref, v_ref, *outs):
        for k in range(tp):
            to = lax.rem(me_ref[0] + k, tp)
            big = pl.ds(pl.multiple_of(to * width, width), width)
            own = pl.ds(pl.multiple_of(to * small, small), small)
            outs[k][:, :width] = q_ref[:, big]
            outs[k][:, width : width + small] = k_ref[:, own]
            outs[k][:, width + small :] = v_ref[:, own]

    total = width + 2 * small
    return pl.pallas_call(
        kernel,
        grid_spec=pltpu.PrefetchScalarGridSpec(
            num_scalar_prefetch=1,
            grid=(1,),
            in_specs=[whole(query.shape), whole(qkeys.shape), whole(qvalues.shape)],
            out_specs=[whole((tokens, total))] * tp,
        ),
        out_shape=[jax.ShapeDtypeStruct((tokens, total), query.dtype)] * tp,
        compiler_params=VMEM,
        name="cut_heads",
    )(me, query, qkeys, qvalues)


def attend(parts_q, received, me, group):
    tp = len(parts_q)
    tokens, total = parts_q[0].shape
    qlen = tp * tokens
    width = group * HD
    bands, top, rows, _ = received.shape
    half = bands // 2
    keys_n = half * top * rows
    all_n = keys_n + qlen
    per = 2
    chunk = 512
    span = 1024
    factor = HD ** (-0.5) * LOG2E
    dims = (((1,), (1,)), ((), ()))

    def lane_max(s, most):
        pieces = [s[:, i : i + HD] for i in range(0, s.shape[1], HD)]
        return functools.reduce(jnp.maximum, pieces if most is None else [most] + pieces)

    def kernel(me_ref, *refs):
        q_refs = refs[:tp]
        k_ref, v_ref, out_ref, scores, values = refs[tp:]
        mine = me_ref[0]
        values[:, HD:] = jnp.ones((all_n, HD), values.dtype)
        values[:keys_n, :HD] = v_ref[...].reshape(keys_n, HD)
        for k in range(tp):
            values[keys_n + k * tokens : keys_n + (k + 1) * tokens, :HD] = q_refs[k][:, width + HD :]

        def position(axis):
            index = lax.broadcasted_iota(jnp.int32, (qlen, qlen), axis)
            owner = lax.bitwise_and(mine - index // tokens + tp, tp - 1)
            return owner * tokens + lax.rem(index, tokens)

        sees = jnp.concatenate([position(0) >= position(1)] * per, axis=0)
        own_keys = jnp.concatenate([q_refs[k][:, width : width + HD] for k in range(tp)], axis=0)

        def score_steps(g):
            heads = [slice((g * per + p) * HD, (g * per + p + 1) * HD) for p in range(per)]
            q = jnp.concatenate([q_refs[k][:, at] for at in heads for k in range(tp)], axis=0)

            def own_step(most):
                s = lax.dot_general(q, own_keys, dims, preferred_element_type=jnp.float32)
                s = jnp.where(sees, s, -jnp.inf)
                scores[g % 2, :, keys_n:] = s
                return lane_max(s, most)

            def step(c, most):
                keys = k_ref[c // (top * rows) : (c + chunk) // (top * rows)].reshape(chunk, HD)
                s = lax.dot_general(q, keys, dims, preferred_element_type=jnp.float32)
                scores[g % 2, :, c : c + chunk] = s
                return lane_max(s, most)

            return [own_step] + [functools.partial(step, c) for c in range(0, keys_n, chunk)]

        most = None
        for step in score_steps(0):
            most = step(most)
        spans = [(c, min(c + span, all_n)) for c in range(0, all_n, span)]
        groups = group // per
        for g in range(groups):
            m = jnp.max(most, axis=1, keepdims=True)
            steps = score_steps(g + 1) if g + 1 < groups else []
            most, total_o, done = None, None, 0
            for i, (lo, hi) in enumerate(spans):
                upto = -(-len(steps) * (i + 1) // len(spans))
                for step in steps[done:upto]:
                    most = step(most)
                done = upto
                w = jnp.exp2((scores[g % 2, :, lo:hi] - m) * factor).astype(values.dtype)
                o = jnp.dot(w, values[lo:hi], preferred_element_type=jnp.float32)
                total_o = o if total_o is None else total_o + o
            o = (total_o[:, :HD] / total_o[:, HD:]).astype(out_ref.dtype)
            for p in range(per):
                for k in range(tp):
                    owner = lax.bitwise_and(mine - k + tp, tp - 1)
                    at = p * qlen + k * tokens
                    out_ref[owner, :, (g * per + p) * HD : (g * per + p + 1) * HD] = o[at : at + tokens]

    return pl.pallas_call(
        kernel,
        grid_spec=pltpu.PrefetchScalarGridSpec(
            num_scalar_prefetch=1,
            grid=(1,),
            in_specs=[whole((tokens, total))] * tp
            + [
                pl.BlockSpec((half, top, rows, HD), lambda s, *_: (0, 0, 0, 0)),
                pl.BlockSpec((half, top, rows, HD), lambda s, *_: (1, 0, 0, 0)),
            ],
            out_specs=whole((tp, tokens, width)),
            scratch_shapes=[
                pltpu.VMEM((2, per * qlen, all_n), jnp.float32),
                pltpu.VMEM((all_n, 2 * HD), jnp.bfloat16),
            ],
        ),
        out_shape=jax.ShapeDtypeStruct((tp, tokens, width), jnp.bfloat16),
        compiler_params=VMEM,
        cost_estimate=pl.CostEstimate(
            flops=4 * group * qlen * all_n * HD,
            bytes_accessed=2 * keys_n * HD * 2,
            transcendentals=group * qlen * all_n,
        ),
        name="attend",
    )(me, *parts_q, received, received)


def join_heads(back):
    groups, tokens, width = back.shape

    def kernel(in_ref, out_ref, sems):
        copies = [
            pltpu.make_async_copy(in_ref.at[g], out_ref.at[0, :, pl.ds(g * width, width)], sems.at[g])
            for g in range(groups)
        ]
        for copy in copies:
            copy.start()
        for copy in copies:
            copy.wait()

    return pl.pallas_call(
        kernel,
        in_specs=[pl.BlockSpec(memory_space=pltpu.VMEM)],
        out_specs=pl.BlockSpec(memory_space=pl.ANY),
        scratch_shapes=[pltpu.SemaphoreType.DMA((groups,))],
        out_shape=jax.ShapeDtypeStruct((1, tokens, groups * width), back.dtype),
        compiler_params=VMEM,
        name="join_heads",
    )(back)


def solution(mesh):
    parts, tp = mesh.shape["cache"], mesh.shape["tp"]

    def local(query, qkeys, qvalues, cache_keys, cache_values, lists):
        at_tp = lax.axis_index("tp").reshape(1).astype(jnp.int32)
        owned = cache_keys.shape[0]
        group = query.shape[2] // qkeys.shape[2]

        top = lists.shape[1]
        bands = cut_bands(cache_keys, cache_values, lists, parts)
        bands = lax.all_to_all(bands, "cache", split_axis=0, concat_axis=0, tiled=True)
        seen = bands[:, owned * ROWS, :top].astype(jnp.int32)
        cuts = cut_heads(query[0], qkeys[0], qvalues[0], at_tp, tp)
        parts_q = [cuts[0]] + [
            lax.ppermute(cuts[k], "tp", [(d, (d + k) % tp) for d in range(tp)]) for k in range(1, tp)
        ]
        picked = pick_rows(bands, seen, owned)
        received = lax.all_to_all(picked, "cache", split_axis=0, concat_axis=0, tiled=True)
        result = attend(parts_q, received, at_tp, group)
        back = lax.all_to_all(result, "tp", split_axis=0, concat_axis=0, tiled=True)
        return join_heads(back)

    return jax.shard_map(
        local,
        mesh=mesh,
        in_specs=(
            P("cache", "tp", None),
            P("cache", "tp", None),
            P("cache", "tp", None),
            P("cache", None, "tp"),
            P("cache", None, "tp"),
            P("cache", None),
        ),
        out_specs=P("cache", "tp", None),
        check_vma=False,
    )
```

```python
import functools

import jax
import jax.numpy as jnp
import numpy as np
from jax import lax
from jax.experimental import pallas as pl
from jax.experimental.pallas import tpu as pltpu
from jax.sharding import PartitionSpec as P

HD = 128
EXTRA = 8
ROWS = 16
LOG2E = 1.4426950408889634
VMEM = pltpu.CompilerParams(vmem_limit_bytes=48 * 1024 * 1024)


def whole(shape):
    return pl.BlockSpec(shape, lambda *_: (0,) * len(shape))


def cut_bands(cache_keys, cache_values, lists, parts):
    owned, plen, width = cache_keys.shape
    half = parts // 2
    rows = owned * ROWS
    top = lists.shape[1]
    pieces = 4
    part = plen // pieces

    def kernel(lists_ref, k_ref, v_ref, out_ref, list_buf, bufs, list_sem, sems):
        list_copy = pltpu.make_async_copy(lists_ref, list_buf, list_sem)
        list_copy.start()
        copies = {}
        for i in range(owned):
            for side, ref in enumerate((k_ref, v_ref)):
                for n in range(pieces):
                    at = pl.ds(n * part, part)
                    copy = pltpu.make_async_copy(ref.at[i, at], bufs.at[side, i, at], sems.at[side, i, n])
                    copy.start()
                    copies[side, i, n] = copy
        list_copy.wait()
        lane = lax.broadcasted_iota(jnp.int32, (top, width), 1)
        spread = lax.rem(lane, top) == lax.broadcasted_iota(jnp.int32, (top, width), 0)
        note = jnp.dot(
            list_buf[...].astype(jnp.bfloat16), spread.astype(jnp.bfloat16), preferred_element_type=jnp.float32
        )
        out_ref[:, rows:] = jnp.broadcast_to(note.astype(out_ref.dtype)[None], (parts, EXTRA, width))
        for i in range(owned):
            at = slice(i * ROWS, (i + 1) * ROWS)
            for side in range(2):
                for n in range(pieces):
                    copies[side, i, n].wait()
                out_ref[side * half : (side + 1) * half, at] = bufs[side, i].reshape(half, ROWS, width)

    return pl.pallas_call(
        kernel,
        in_specs=[pl.BlockSpec(memory_space=pltpu.HBM)] * 3,
        out_specs=pl.BlockSpec(memory_space=pltpu.VMEM),
        scratch_shapes=[
            pltpu.VMEM(lists.shape, lists.dtype),
            pltpu.VMEM((2, owned, plen, width), cache_keys.dtype),
            pltpu.SemaphoreType.DMA,
            pltpu.SemaphoreType.DMA((2, owned, pieces)),
        ],
        out_shape=jax.ShapeDtypeStruct((parts, rows + EXTRA, width), cache_keys.dtype),
        compiler_params=pltpu.CompilerParams(vmem_limit_bytes=40 * 1024 * 1024),
        name="cut_bands",
    )(
        pltpu.with_memory_space_constraint(lists, pltpu.HBM),
        pltpu.with_memory_space_constraint(cache_keys, pltpu.HBM),
        pltpu.with_memory_space_constraint(cache_values, pltpu.HBM),
    )


def pick_rows(bands, lists, owned, top):
    parts, _, width = bands.shape
    each = lists.shape[1] // top
    assert owned & (owned - 1) == 0
    shift = owned.bit_length() - 1

    steps = 16
    share = parts // steps

    def kernel(lists_ref, bands_ref, out_ref, buf, sems):
        def one(d, carry):
            found = []
            for j in range(top):
                passage = lists_ref[lax.div(d, each), lax.rem(d, each) * top + j]
                at = pl.multiple_of(lax.bitwise_and(passage, owned - 1) * ROWS, ROWS)
                found.append(bands_ref[lax.shift_right_logical(passage, shift), pl.ds(at, ROWS)])
            for j in range(top):
                buf[d, j] = found[j]
            return carry

        copies = []
        for step in range(steps):
            lax.fori_loop(step * share, (step + 1) * share, one, 0, unroll=4)
            at = pl.ds(step * share, share)
            copies.append(pltpu.make_async_copy(buf.at[at], out_ref.at[at], sems.at[step]))
            copies[-1].start()
        for copy in copies:
            copy.wait()

    return pl.pallas_call(
        kernel,
        in_specs=[pl.BlockSpec(memory_space=pltpu.SMEM), pl.BlockSpec(memory_space=pltpu.VMEM)],
        out_specs=pl.BlockSpec(memory_space=pl.ANY),
        scratch_shapes=[
            pltpu.VMEM((parts, top, ROWS, width), bands.dtype),
            pltpu.SemaphoreType.DMA((steps,)),
        ],
        out_shape=jax.ShapeDtypeStruct((parts, top, ROWS, width), bands.dtype),
        compiler_params=VMEM,
        name="pick_rows",
    )(lists, bands)


def cut_heads(query, qkeys, qvalues, me, tp):
    tokens, width = query.shape[0], query.shape[1] // tp
    small = qkeys.shape[1] // tp

    def kernel(me_ref, q_ref, k_ref, v_ref, *outs):
        for k in range(tp):
            to = lax.rem(me_ref[0] + k, tp)
            big = pl.ds(pl.multiple_of(to * width, width), width)
            own = pl.ds(pl.multiple_of(to * small, small), small)
            outs[k][:, :width] = q_ref[:, big]
            outs[k][:, width : width + small] = k_ref[:, own]
            outs[k][:, width + small :] = v_ref[:, own]

    total = width + 2 * small
    return pl.pallas_call(
        kernel,
        grid_spec=pltpu.PrefetchScalarGridSpec(
            num_scalar_prefetch=1,
            grid=(1,),
            in_specs=[whole(query.shape), whole(qkeys.shape), whole(qvalues.shape)],
            out_specs=[whole((tokens, total))] * tp,
        ),
        out_shape=[jax.ShapeDtypeStruct((tokens, total), query.dtype)] * tp,
        compiler_params=VMEM,
        name="cut_heads",
    )(me, query, qkeys, qvalues)


def attend(parts_q, received, me, group):
    tp = len(parts_q)
    tokens, total = parts_q[0].shape
    qlen = tp * tokens
    width = group * HD
    bands, top, rows, _ = received.shape
    half = bands // 2
    keys_n = half * top * rows
    all_n = keys_n + qlen
    per = 2
    chunk = 512
    span = 1024
    factor = HD ** (-0.5) * LOG2E
    dims = (((1,), (1,)), ((), ()))

    def lane_max(s, most):
        pieces = [s[:, i : i + HD] for i in range(0, s.shape[1], HD)]
        return functools.reduce(jnp.maximum, pieces if most is None else [most] + pieces)

    def kernel(me_ref, *refs):
        q_refs = refs[:tp]
        k_ref, v_ref, out_ref, scores, values = refs[tp:]
        mine = me_ref[0]
        values[:, HD:] = jnp.ones((all_n, HD), values.dtype)
        values[:keys_n, :HD] = v_ref[...].reshape(keys_n, HD)
        for k in range(tp):
            values[keys_n + k * tokens : keys_n + (k + 1) * tokens, :HD] = q_refs[k][:, width + HD :]

        def position(axis):
            index = lax.broadcasted_iota(jnp.int32, (qlen, qlen), axis)
            owner = lax.bitwise_and(mine - index // tokens + tp, tp - 1)
            return owner * tokens + lax.rem(index, tokens)

        sees = jnp.concatenate([position(0) >= position(1)] * per, axis=0)
        own_keys = jnp.concatenate([q_refs[k][:, width : width + HD] for k in range(tp)], axis=0)

        def score_steps(g):
            heads = [slice((g * per + p) * HD, (g * per + p + 1) * HD) for p in range(per)]
            q = jnp.concatenate([q_refs[k][:, at] for at in heads for k in range(tp)], axis=0)

            def own_step(most):
                s = lax.dot_general(q, own_keys, dims, preferred_element_type=jnp.float32)
                s = jnp.where(sees, s, -jnp.inf)
                scores[g % 2, :, keys_n:] = s
                return lane_max(s, most)

            def step(c, most):
                keys = k_ref[c // (top * rows) : (c + chunk) // (top * rows)].reshape(chunk, HD)
                s = lax.dot_general(q, keys, dims, preferred_element_type=jnp.float32)
                scores[g % 2, :, c : c + chunk] = s
                return lane_max(s, most)

            return [own_step] + [functools.partial(step, c) for c in range(0, keys_n, chunk)]

        most = None
        for step in score_steps(0):
            most = step(most)
        spans = [(c, min(c + span, all_n)) for c in range(0, all_n, span)]
        groups = group // per
        for g in range(groups):
            m = jnp.max(most, axis=1, keepdims=True)
            steps = score_steps(g + 1) if g + 1 < groups else []
            most, total_o, done = None, None, 0
            for i, (lo, hi) in enumerate(spans):
                upto = -(-len(steps) * (i + 1) // len(spans))
                for step in steps[done:upto]:
                    most = step(most)
                done = upto
                w = jnp.exp2((scores[g % 2, :, lo:hi] - m) * factor).astype(values.dtype)
                o = jnp.dot(w, values[lo:hi], preferred_element_type=jnp.float32)
                total_o = o if total_o is None else total_o + o
            o = (total_o[:, :HD] / total_o[:, HD:]).astype(out_ref.dtype)
            for p in range(per):
                for k in range(tp):
                    owner = lax.bitwise_and(mine - k + tp, tp - 1)
                    at = p * qlen + k * tokens
                    out_ref[owner, :, (g * per + p) * HD : (g * per + p + 1) * HD] = o[at : at + tokens]

    return pl.pallas_call(
        kernel,
        grid_spec=pltpu.PrefetchScalarGridSpec(
            num_scalar_prefetch=1,
            grid=(1,),
            in_specs=[whole((tokens, total))] * tp
            + [
                pl.BlockSpec((half, top, rows, HD), lambda s, *_: (0, 0, 0, 0)),
                pl.BlockSpec((half, top, rows, HD), lambda s, *_: (1, 0, 0, 0)),
            ],
            out_specs=whole((tp, tokens, width)),
            scratch_shapes=[
                pltpu.VMEM((2, per * qlen, all_n), jnp.float32),
                pltpu.VMEM((all_n, 2 * HD), jnp.bfloat16),
            ],
        ),
        out_shape=jax.ShapeDtypeStruct((tp, tokens, width), jnp.bfloat16),
        compiler_params=VMEM,
        cost_estimate=pl.CostEstimate(
            flops=4 * group * qlen * all_n * HD,
            bytes_accessed=2 * keys_n * HD * 2,
            transcendentals=group * qlen * all_n,
        ),
        name="attend",
    )(me, *parts_q, received, received)


def join_heads(back):
    groups, tokens, width = back.shape

    def kernel(in_ref, out_ref, sems):
        copies = [
            pltpu.make_async_copy(in_ref.at[g], out_ref.at[0, :, pl.ds(g * width, width)], sems.at[g])
            for g in range(groups)
        ]
        for copy in copies:
            copy.start()
        for copy in copies:
            copy.wait()

    return pl.pallas_call(
        kernel,
        in_specs=[pl.BlockSpec(memory_space=pltpu.VMEM)],
        out_specs=pl.BlockSpec(memory_space=pl.ANY),
        scratch_shapes=[pltpu.SemaphoreType.DMA((groups,))],
        out_shape=jax.ShapeDtypeStruct((1, tokens, groups * width), back.dtype),
        compiler_params=VMEM,
        name="join_heads",
    )(back)


def solution(mesh):
    parts, tp = mesh.shape["cache"], mesh.shape["tp"]

    def local(query, qkeys, qvalues, cache_keys, cache_values, lists):
        at_tp = lax.axis_index("tp").reshape(1).astype(jnp.int32)
        owned = cache_keys.shape[0]
        group = query.shape[2] // qkeys.shape[2]

        top = lists.shape[1]
        bands = cut_bands(cache_keys, cache_values, lists, parts)
        bands = lax.all_to_all(bands, "cache", split_axis=0, concat_axis=0, tiled=True)
        lanes = bands.shape[2]
        each = lanes // top
        mine = np.arange(parts)[:, None] % each == np.arange(lanes)[None, :] // top
        seen = jnp.where(mine, bands[:, owned * ROWS], 0).astype(jnp.int32).reshape(parts // each, each, lanes).sum(1)
        cuts = cut_heads(query[0], qkeys[0], qvalues[0], at_tp, tp)
        parts_q = [cuts[0]] + [
            lax.ppermute(cuts[k], "tp", [(d, (d + k) % tp) for d in range(tp)]) for k in range(1, tp)
        ]
        picked = pick_rows(bands, seen, owned, top)
        received = lax.all_to_all(picked, "cache", split_axis=0, concat_axis=0, tiled=True)
        result = attend(parts_q, received, at_tp, group)
        back = lax.all_to_all(result, "tp", split_axis=0, concat_axis=0, tiled=True)
        return join_heads(back)

    return jax.shard_map(
        local,
        mesh=mesh,
        in_specs=(
            P("cache", "tp", None),
            P("cache", "tp", None),
            P("cache", "tp", None),
            P("cache", None, "tp"),
            P("cache", None, "tp"),
            P("cache", None),
        ),
        out_specs=P("cache", "tp", None),
        check_vma=False,
    )
```

```python
import functools

import jax
import jax.numpy as jnp
import numpy as np
from jax import lax
from jax.experimental import pallas as pl
from jax.experimental.pallas import tpu as pltpu
from jax.sharding import PartitionSpec as P

HD = 128
EXTRA = 8
ROWS = 16
LOG2E = 1.4426950408889634
VMEM = pltpu.CompilerParams(vmem_limit_bytes=48 * 1024 * 1024)


def whole(shape):
    return pl.BlockSpec(shape, lambda *_: (0,) * len(shape))


def cut_bands(cache_keys, cache_values, lists, parts):
    owned, plen, width = cache_keys.shape
    half = parts // 2
    rows = owned * ROWS
    top = lists.shape[1]
    pieces = 1
    part = plen // pieces

    def kernel(lists_ref, k_ref, v_ref, out_ref, note_ref, list_buf, bufs, list_sem, sems):
        list_copy = pltpu.make_async_copy(lists_ref, list_buf, list_sem)
        list_copy.start()
        copies = {}
        for i in range(owned):
            for side, ref in enumerate((k_ref, v_ref)):
                for n in range(pieces):
                    at = pl.ds(n * part, part)
                    copy = pltpu.make_async_copy(ref.at[i, at], bufs.at[side, i, at], sems.at[side, i, n])
                    copy.start()
                    copies[side, i, n] = copy
        list_copy.wait()
        lane = lax.broadcasted_iota(jnp.int32, (top, width), 1)
        spread = lax.rem(lane, top) == lax.broadcasted_iota(jnp.int32, (top, width), 0)
        note = jnp.dot(
            list_buf[...].astype(jnp.bfloat16), spread.astype(jnp.bfloat16), preferred_element_type=jnp.float32
        )
        note_ref[...] = jnp.broadcast_to(note, (ROWS, width)).astype(note_ref.dtype)
        for i in range(owned):
            at = slice(i * ROWS, (i + 1) * ROWS)
            for side in range(2):
                for n in range(pieces):
                    copies[side, i, n].wait()
                out_ref[side * half : (side + 1) * half, at] = bufs[side, i].reshape(half, ROWS, width)

    return pl.pallas_call(
        kernel,
        in_specs=[pl.BlockSpec(memory_space=pltpu.HBM)] * 3,
        out_specs=[pl.BlockSpec(memory_space=pltpu.VMEM)] * 2,
        scratch_shapes=[
            pltpu.VMEM(lists.shape, lists.dtype),
            pltpu.VMEM((2, owned, plen, width), cache_keys.dtype),
            pltpu.SemaphoreType.DMA,
            pltpu.SemaphoreType.DMA((2, owned, pieces)),
        ],
        out_shape=[
            jax.ShapeDtypeStruct((parts, rows + EXTRA, width), cache_keys.dtype),
            jax.ShapeDtypeStruct((ROWS, width), cache_keys.dtype),
        ],
        compiler_params=pltpu.CompilerParams(vmem_limit_bytes=40 * 1024 * 1024),
        name="cut_bands",
    )(
        pltpu.with_memory_space_constraint(lists, pltpu.HBM),
        pltpu.with_memory_space_constraint(cache_keys, pltpu.HBM),
        pltpu.with_memory_space_constraint(cache_values, pltpu.HBM),
    )


def pick_rows(bands, lists, owned, top):
    parts, _, width = bands.shape
    each = lists.shape[1] // top
    assert owned & (owned - 1) == 0
    shift = owned.bit_length() - 1

    steps = 8
    share = parts // steps

    def kernel(lists_ref, bands_ref, out_ref, buf, sems):
        def one(d, carry):
            found = []
            for j in range(top):
                passage = lists_ref[lax.div(d, each), lax.rem(d, each) * top + j]
                at = pl.multiple_of(lax.bitwise_and(passage, owned - 1) * ROWS, ROWS)
                found.append(bands_ref[lax.shift_right_logical(passage, shift), pl.ds(at, ROWS)])
            for j in range(top):
                buf[d, j] = found[j]
            return carry

        copies = []
        for step in range(steps):
            lax.fori_loop(step * share, (step + 1) * share, one, 0, unroll=8)
            at = pl.ds(step * share, share)
            copies.append(pltpu.make_async_copy(buf.at[at], out_ref.at[at], sems.at[step]))
            copies[-1].start()
        for copy in copies:
            copy.wait()

    return pl.pallas_call(
        kernel,
        in_specs=[pl.BlockSpec(memory_space=pltpu.SMEM), pl.BlockSpec(memory_space=pltpu.VMEM)],
        out_specs=pl.BlockSpec(memory_space=pl.ANY),
        scratch_shapes=[
            pltpu.VMEM((parts, top, ROWS, width), bands.dtype),
            pltpu.SemaphoreType.DMA((steps,)),
        ],
        out_shape=jax.ShapeDtypeStruct((parts, top, ROWS, width), bands.dtype),
        compiler_params=VMEM,
        name="pick_rows",
    )(lists, bands)


def cut_heads(query, qkeys, qvalues, me, tp):
    tokens, width = query.shape[0], query.shape[1] // tp
    small = qkeys.shape[1] // tp

    def kernel(me_ref, q_ref, k_ref, v_ref, *outs):
        for k in range(tp):
            to = lax.rem(me_ref[0] + k, tp)
            big = pl.ds(pl.multiple_of(to * width, width), width)
            own = pl.ds(pl.multiple_of(to * small, small), small)
            outs[k][:, :width] = q_ref[:, big]
            outs[k][:, width : width + small] = k_ref[:, own]
            outs[k][:, width + small :] = v_ref[:, own]

    total = width + 2 * small
    return pl.pallas_call(
        kernel,
        grid_spec=pltpu.PrefetchScalarGridSpec(
            num_scalar_prefetch=1,
            grid=(1,),
            in_specs=[whole(query.shape), whole(qkeys.shape), whole(qvalues.shape)],
            out_specs=[whole((tokens, total))] * tp,
        ),
        out_shape=[jax.ShapeDtypeStruct((tokens, total), query.dtype)] * tp,
        compiler_params=VMEM,
        name="cut_heads",
    )(me, query, qkeys, qvalues)


def attend(parts_q, received, me, group):
    tp = len(parts_q)
    tokens, total = parts_q[0].shape
    qlen = tp * tokens
    width = group * HD
    bands, top, rows, _ = received.shape
    half = bands // 2
    keys_n = half * top * rows
    all_n = keys_n + qlen
    per = 1
    chunk = 512
    span = 1024
    factor = HD ** (-0.5) * LOG2E
    dims = (((1,), (1,)), ((), ()))

    def lane_max(s, most):
        pieces = [s[:, i : i + HD] for i in range(0, s.shape[1], HD)]
        return functools.reduce(jnp.maximum, pieces if most is None else [most] + pieces)

    def kernel(me_ref, *refs):
        q_refs = refs[:tp]
        k_ref, v_ref, out_ref, scores, values = refs[tp:]
        mine = me_ref[0]
        values[:, HD:] = jnp.ones((all_n, HD), values.dtype)
        values[:keys_n, :HD] = v_ref[...].reshape(keys_n, HD)
        for k in range(tp):
            values[keys_n + k * tokens : keys_n + (k + 1) * tokens, :HD] = q_refs[k][:, width + HD :]

        def position(axis):
            index = lax.broadcasted_iota(jnp.int32, (qlen, qlen), axis)
            owner = lax.bitwise_and(mine - index // tokens + tp, tp - 1)
            return owner * tokens + lax.rem(index, tokens)

        sees = jnp.concatenate([position(0) >= position(1)] * per, axis=0)
        own_keys = jnp.concatenate([q_refs[k][:, width : width + HD] for k in range(tp)], axis=0)

        def score_steps(g):
            heads = [slice((g * per + p) * HD, (g * per + p + 1) * HD) for p in range(per)]
            q = jnp.concatenate([q_refs[k][:, at] for at in heads for k in range(tp)], axis=0)

            def own_step(most):
                s = lax.dot_general(q, own_keys, dims, preferred_element_type=jnp.float32)
                s = jnp.where(sees, s, -jnp.inf)
                scores[g % 2, :, keys_n:] = s
                return lane_max(s, most)

            def step(c, most):
                keys = k_ref[c // (top * rows) : (c + chunk) // (top * rows)].reshape(chunk, HD)
                s = lax.dot_general(q, keys, dims, preferred_element_type=jnp.float32)
                scores[g % 2, :, c : c + chunk] = s
                return lane_max(s, most)

            return [own_step] + [functools.partial(step, c) for c in range(0, keys_n, chunk)]

        most = None
        for step in score_steps(0):
            most = step(most)
        spans = [(c, min(c + span, all_n)) for c in range(0, all_n, span)]
        groups = group // per
        for g in range(groups):
            m = jnp.max(most, axis=1, keepdims=True)
            steps = score_steps(g + 1) if g + 1 < groups else []
            most, total_o, done = None, None, 0
            for i, (lo, hi) in enumerate(spans):
                upto = -(-len(steps) * (i + 1) // len(spans))
                for step in steps[done:upto]:
                    most = step(most)
                done = upto
                w = jnp.exp2((scores[g % 2, :, lo:hi] - m) * factor).astype(values.dtype)
                o = jnp.dot(w, values[lo:hi], preferred_element_type=jnp.float32)
                total_o = o if total_o is None else total_o + o
            o = (total_o[:, :HD] / total_o[:, HD:]).astype(out_ref.dtype)
            for p in range(per):
                for k in range(tp):
                    owner = lax.bitwise_and(mine - k + tp, tp - 1)
                    at = p * qlen + k * tokens
                    out_ref[owner, :, (g * per + p) * HD : (g * per + p + 1) * HD] = o[at : at + tokens]

    return pl.pallas_call(
        kernel,
        grid_spec=pltpu.PrefetchScalarGridSpec(
            num_scalar_prefetch=1,
            grid=(1,),
            in_specs=[whole((tokens, total))] * tp
            + [
                pl.BlockSpec((half, top, rows, HD), lambda s, *_: (0, 0, 0, 0)),
                pl.BlockSpec((half, top, rows, HD), lambda s, *_: (1, 0, 0, 0)),
            ],
            out_specs=whole((tp, tokens, width)),
            scratch_shapes=[
                pltpu.VMEM((2, per * qlen, all_n), jnp.float32),
                pltpu.VMEM((all_n, 2 * HD), jnp.bfloat16),
            ],
        ),
        out_shape=jax.ShapeDtypeStruct((tp, tokens, width), jnp.bfloat16),
        compiler_params=VMEM,
        cost_estimate=pl.CostEstimate(
            flops=4 * group * qlen * all_n * HD,
            bytes_accessed=2 * keys_n * HD * 2,
            transcendentals=group * qlen * all_n,
        ),
        name="attend",
    )(me, *parts_q, received, received)


def join_heads(back):
    groups, tokens, width = back.shape

    def kernel(in_ref, out_ref, sems):
        copies = [
            pltpu.make_async_copy(in_ref.at[g], out_ref.at[0, :, pl.ds(g * width, width)], sems.at[g])
            for g in range(groups)
        ]
        for copy in copies:
            copy.start()
        for copy in copies:
            copy.wait()

    return pl.pallas_call(
        kernel,
        in_specs=[pl.BlockSpec(memory_space=pltpu.VMEM)],
        out_specs=pl.BlockSpec(memory_space=pl.ANY),
        scratch_shapes=[pltpu.SemaphoreType.DMA((groups,))],
        out_shape=jax.ShapeDtypeStruct((1, tokens, groups * width), back.dtype),
        compiler_params=VMEM,
        name="join_heads",
    )(back)


def solution(mesh):
    parts, tp = mesh.shape["cache"], mesh.shape["tp"]

    def local(query, qkeys, qvalues, cache_keys, cache_values, lists):
        at_tp = lax.axis_index("tp").reshape(1).astype(jnp.int32)
        owned = cache_keys.shape[0]
        group = query.shape[2] // qkeys.shape[2]

        top = lists.shape[1]
        bands, note = cut_bands(cache_keys, cache_values, lists, parts)
        bands = bands.at[:, owned * ROWS :].set(note[None, :EXTRA])
        bands = lax.all_to_all(bands, "cache", split_axis=0, concat_axis=0, tiled=True)
        lanes = bands.shape[2]
        each = lanes // top
        mine = np.arange(parts)[:, None] % each == np.arange(lanes)[None, :] // top
        seen = jnp.where(mine, bands[:, owned * ROWS], 0).astype(jnp.int32).reshape(parts // each, each, lanes).sum(1)
        cuts = cut_heads(query[0], qkeys[0], qvalues[0], at_tp, tp)
        parts_q = [cuts[0]] + [
            lax.ppermute(cuts[k], "tp", [(d, (d + k) % tp) for d in range(tp)]) for k in range(1, tp)
        ]
        picked = pick_rows(bands, seen, owned, top)
        received = lax.all_to_all(picked, "cache", split_axis=0, concat_axis=0, tiled=True)
        result = attend(parts_q, received, at_tp, group)
        back = lax.all_to_all(result, "tp", split_axis=0, concat_axis=0, tiled=True)
        return join_heads(back)

    return jax.shard_map(
        local,
        mesh=mesh,
        in_specs=(
            P("cache", "tp", None),
            P("cache", "tp", None),
            P("cache", "tp", None),
            P("cache", None, "tp"),
            P("cache", None, "tp"),
            P("cache", None),
        ),
        out_specs=P("cache", "tp", None),
        check_vma=False,
    )
```

```python
import functools

import jax
import jax.numpy as jnp
import numpy as np
from jax import lax
from jax.experimental import pallas as pl
from jax.experimental.pallas import tpu as pltpu
from jax.sharding import PartitionSpec as P

HD = 128
EXTRA = 8
ROWS = 16
LOG2E = 1.4426950408889634
LARGE = 1e30
VMEM = pltpu.CompilerParams(vmem_limit_bytes=48 * 1024 * 1024)


def whole(shape):
    return pl.BlockSpec(shape, lambda *_: (0,) * len(shape))


def cut_bands(cache_keys, cache_values, lists, parts):
    owned, plen, width = cache_keys.shape
    half = parts // 2
    rows = owned * ROWS
    top = lists.shape[1]
    pieces = 1
    part = plen // pieces

    def kernel(lists_ref, k_ref, v_ref, out_ref, note_ref, list_buf, bufs, list_sem, sems):
        list_copy = pltpu.make_async_copy(lists_ref, list_buf, list_sem)
        list_copy.start()
        copies = {}
        for i in range(owned):
            for side, ref in enumerate((k_ref, v_ref)):
                for n in range(pieces):
                    at = pl.ds(n * part, part)
                    copy = pltpu.make_async_copy(ref.at[i, at], bufs.at[side, i, at], sems.at[side, i, n])
                    copy.start()
                    copies[side, i, n] = copy
        list_copy.wait()
        lane = lax.broadcasted_iota(jnp.int32, (top, width), 1)
        spread = lax.rem(lane, top) == lax.broadcasted_iota(jnp.int32, (top, width), 0)
        note = jnp.dot(
            list_buf[...].astype(jnp.bfloat16), spread.astype(jnp.bfloat16), preferred_element_type=jnp.float32
        )
        note_ref[...] = jnp.broadcast_to(note, (ROWS, width)).astype(note_ref.dtype)
        for i in range(owned):
            at = slice(i * ROWS, (i + 1) * ROWS)
            for side in range(2):
                for n in range(pieces):
                    copies[side, i, n].wait()
                out_ref[side * half : (side + 1) * half, at] = bufs[side, i].reshape(half, ROWS, width)

    return pl.pallas_call(
        kernel,
        in_specs=[pl.BlockSpec(memory_space=pltpu.HBM)] * 3,
        out_specs=[pl.BlockSpec(memory_space=pltpu.VMEM)] * 2,
        scratch_shapes=[
            pltpu.VMEM(lists.shape, lists.dtype),
            pltpu.VMEM((2, owned, plen, width), cache_keys.dtype),
            pltpu.SemaphoreType.DMA,
            pltpu.SemaphoreType.DMA((2, owned, pieces)),
        ],
        out_shape=[
            jax.ShapeDtypeStruct((parts, rows + EXTRA, width), cache_keys.dtype),
            jax.ShapeDtypeStruct((ROWS, width), cache_keys.dtype),
        ],
        compiler_params=pltpu.CompilerParams(vmem_limit_bytes=40 * 1024 * 1024),
        name="cut_bands",
    )(
        pltpu.with_memory_space_constraint(lists, pltpu.HBM),
        pltpu.with_memory_space_constraint(cache_keys, pltpu.HBM),
        pltpu.with_memory_space_constraint(cache_values, pltpu.HBM),
    )


def pick_rows(bands, lists, owned, top):
    parts, _, width = bands.shape
    each = lists.shape[1] // top
    assert owned & (owned - 1) == 0
    shift = owned.bit_length() - 1

    steps = 8
    share = parts // steps

    def kernel(lists_ref, bands_ref, out_ref, buf, sems):
        def one(d, carry):
            found = []
            for j in range(top):
                passage = lists_ref[lax.div(d, each), lax.rem(d, each) * top + j]
                at = pl.multiple_of(lax.bitwise_and(passage, owned - 1) * ROWS, ROWS)
                found.append(bands_ref[lax.shift_right_logical(passage, shift), pl.ds(at, ROWS)])
            for j in range(top):
                buf[d, j] = found[j]
            return carry

        copies = []
        for step in range(steps):
            lax.fori_loop(step * share, (step + 1) * share, one, 0, unroll=8)
            at = pl.ds(step * share, share)
            copies.append(pltpu.make_async_copy(buf.at[at], out_ref.at[at], sems.at[step]))
            copies[-1].start()
        for copy in copies:
            copy.wait()

    return pl.pallas_call(
        kernel,
        in_specs=[pl.BlockSpec(memory_space=pltpu.SMEM), pl.BlockSpec(memory_space=pltpu.VMEM)],
        out_specs=pl.BlockSpec(memory_space=pl.ANY),
        scratch_shapes=[
            pltpu.VMEM((parts, top, ROWS, width), bands.dtype),
            pltpu.SemaphoreType.DMA((steps,)),
        ],
        out_shape=jax.ShapeDtypeStruct((parts, top, ROWS, width), bands.dtype),
        compiler_params=VMEM,
        name="pick_rows",
    )(lists, bands)


def cut_heads(query, qkeys, qvalues, me, tp):
    tokens, width = query.shape[0], query.shape[1] // tp
    small = qkeys.shape[1] // tp

    def kernel(me_ref, q_ref, k_ref, v_ref, *outs):
        for k in range(tp):
            to = lax.rem(me_ref[0] + k, tp)
            big = pl.ds(pl.multiple_of(to * width, width), width)
            own = pl.ds(pl.multiple_of(to * small, small), small)
            outs[k][:, :width] = q_ref[:, big]
            outs[k][:, width : width + small] = k_ref[:, own]
            outs[k][:, width + small :] = v_ref[:, own]

    total = width + 2 * small
    return pl.pallas_call(
        kernel,
        grid_spec=pltpu.PrefetchScalarGridSpec(
            num_scalar_prefetch=1,
            grid=(1,),
            in_specs=[whole(query.shape), whole(qkeys.shape), whole(qvalues.shape)],
            out_specs=[whole((tokens, total))] * tp,
        ),
        out_shape=[jax.ShapeDtypeStruct((tokens, total), query.dtype)] * tp,
        compiler_params=VMEM,
        name="cut_heads",
    )(me, query, qkeys, qvalues)


def attend(parts_q, received, me, group):
    tp = len(parts_q)
    tokens, total = parts_q[0].shape
    qlen = tp * tokens
    width = group * HD
    bands, top, rows, _ = received.shape
    half = bands // 2
    keys_n = half * top * rows
    all_n = keys_n + qlen
    chunk = 512
    span = 1024
    factor = HD ** (-0.5) * LOG2E
    dims = (((1,), (1,)), ((), ()))

    def lane_max(s, most):
        pieces = [s[:, i : i + HD] for i in range(0, s.shape[1], HD)]
        return functools.reduce(jnp.maximum, pieces if most is None else [most] + pieces)

    def kernel(me_ref, *refs):
        q_refs = refs[:tp]
        k_ref, v_ref, out_ref, scores, values = refs[tp:]
        mine = me_ref[0]
        values[:, HD:] = jnp.ones((all_n, HD), values.dtype)
        values[:keys_n, :HD] = v_ref[...].reshape(keys_n, HD)
        for k in range(tp):
            values[keys_n + k * tokens : keys_n + (k + 1) * tokens, :HD] = q_refs[k][:, width + HD :]

        def position(axis):
            index = lax.broadcasted_iota(jnp.int32, (qlen, qlen), axis)
            owner = lax.bitwise_and(mine - index // tokens + tp, tp - 1)
            return owner * tokens + lax.rem(index, tokens)

        sees = position(0) >= position(1)
        own_keys = jnp.concatenate([q_refs[k][:, width : width + HD] for k in range(tp)], axis=0)

        def columns(g):
            return pl.ds(pl.multiple_of(g * HD, HD), HD)

        def queries(at):
            return jnp.concatenate([q_refs[k][:, at] for k in range(tp)], axis=0)

        def own_scores(q):
            return jnp.where(sees, lax.dot_general(q, own_keys, dims, preferred_element_type=jnp.float32), -jnp.inf)

        def listed_scores(q, c):
            keys = k_ref[c // (top * rows) : (c + chunk) // (top * rows)].reshape(chunk, HD)
            return lax.dot_general(q, keys, dims, preferred_element_type=jnp.float32)

        def weigh(s, m):
            return jnp.exp2((s - m) * factor).astype(values.dtype)

        def add_up(w, lo):
            return jnp.dot(w, values[lo : lo + w.shape[1]], preferred_element_type=jnp.float32)

        def store(at, sums):
            o = (sums[:, :HD] / sums[:, HD:]).astype(out_ref.dtype)
            for k in range(tp):
                owner = lax.bitwise_and(mine - k + tp, tp - 1)
                out_ref[owner, :, at] = o[k * tokens : (k + 1) * tokens]

        def begin(g):
            q = queries(slice(g * HD, (g + 1) * HD))
            s = own_scores(q)
            return q, s, jnp.max(lane_max(s, None), axis=1, keepdims=True)

        following = begin(0)
        too_large = jnp.zeros((qlen, HD), jnp.float32)
        for g in range(group):
            q, s, m = following
            sums = add_up(weigh(s, m), keys_n)
            for lo in range(0, keys_n, span):
                w = [weigh(listed_scores(q, c), m) for c in range(lo, lo + span, chunk)]
                sums = sums + add_up(jnp.concatenate(w, axis=1), lo)
                if lo == keys_n // 2 and g + 1 < group:
                    following = begin(g + 1)
            too_large = jnp.maximum(too_large, jnp.where(sums[:, HD:] < LARGE, 0.0, 1.0))
            store(slice(g * HD, (g + 1) * HD), sums)

        @pl.when(jnp.max(too_large) > 0.0)
        def _():
            def again(g, carry):
                q = queries(columns(g))
                s = own_scores(q)
                scores[:, keys_n:] = s
                most = lane_max(s, None)
                for c in range(0, keys_n, chunk):
                    s = listed_scores(q, c)
                    scores[:, c : c + chunk] = s
                    most = lane_max(s, most)
                m = jnp.max(most, axis=1, keepdims=True)
                sums = add_up(weigh(scores[:, keys_n:], m), keys_n)
                for c in range(0, keys_n, chunk):
                    sums = sums + add_up(weigh(scores[:, c : c + chunk], m), c)
                store(columns(g), sums)
                return carry

            lax.fori_loop(0, group, again, 0)

    return pl.pallas_call(
        kernel,
        grid_spec=pltpu.PrefetchScalarGridSpec(
            num_scalar_prefetch=1,
            grid=(1,),
            in_specs=[whole((tokens, total))] * tp
            + [
                pl.BlockSpec((half, top, rows, HD), lambda s, *_: (0, 0, 0, 0)),
                pl.BlockSpec((half, top, rows, HD), lambda s, *_: (1, 0, 0, 0)),
            ],
            out_specs=whole((tp, tokens, width)),
            scratch_shapes=[
                pltpu.VMEM((qlen, all_n), jnp.float32),
                pltpu.VMEM((all_n, 2 * HD), jnp.bfloat16),
            ],
        ),
        out_shape=jax.ShapeDtypeStruct((tp, tokens, width), jnp.bfloat16),
        compiler_params=VMEM,
        cost_estimate=pl.CostEstimate(
            flops=4 * group * qlen * all_n * HD,
            bytes_accessed=2 * keys_n * HD * 2,
            transcendentals=group * qlen * all_n,
        ),
        name="attend",
    )(me, *parts_q, received, received)


def join_heads(back):
    groups, tokens, width = back.shape

    def kernel(in_ref, out_ref, sems):
        copies = [
            pltpu.make_async_copy(in_ref.at[g], out_ref.at[0, :, pl.ds(g * width, width)], sems.at[g])
            for g in range(groups)
        ]
        for copy in copies:
            copy.start()
        for copy in copies:
            copy.wait()

    return pl.pallas_call(
        kernel,
        in_specs=[pl.BlockSpec(memory_space=pltpu.VMEM)],
        out_specs=pl.BlockSpec(memory_space=pl.ANY),
        scratch_shapes=[pltpu.SemaphoreType.DMA((groups,))],
        out_shape=jax.ShapeDtypeStruct((1, tokens, groups * width), back.dtype),
        compiler_params=VMEM,
        name="join_heads",
    )(back)


def solution(mesh):
    parts, tp = mesh.shape["cache"], mesh.shape["tp"]

    def local(query, qkeys, qvalues, cache_keys, cache_values, lists):
        at_tp = lax.axis_index("tp").reshape(1).astype(jnp.int32)
        owned = cache_keys.shape[0]
        group = query.shape[2] // qkeys.shape[2]

        top = lists.shape[1]
        bands, note = cut_bands(cache_keys, cache_values, lists, parts)
        bands = bands.at[:, owned * ROWS :].set(note[None, :EXTRA])
        bands = lax.all_to_all(bands, "cache", split_axis=0, concat_axis=0, tiled=True)
        lanes = bands.shape[2]
        each = lanes // top
        mine = np.arange(parts)[:, None] % each == np.arange(lanes)[None, :] // top
        seen = jnp.where(mine, bands[:, owned * ROWS], 0).astype(jnp.int32).reshape(parts // each, each, lanes).sum(1)
        cuts = cut_heads(query[0], qkeys[0], qvalues[0], at_tp, tp)
        parts_q = [cuts[0]] + [
            lax.ppermute(cuts[k], "tp", [(d, (d + k) % tp) for d in range(tp)]) for k in range(1, tp)
        ]
        picked = pick_rows(bands, seen, owned, top)
        received = lax.all_to_all(picked, "cache", split_axis=0, concat_axis=0, tiled=True)
        result = attend(parts_q, received, at_tp, group)
        back = lax.all_to_all(result, "tp", split_axis=0, concat_axis=0, tiled=True)
        return join_heads(back)

    return jax.shard_map(
        local,
        mesh=mesh,
        in_specs=(
            P("cache", "tp", None),
            P("cache", "tp", None),
            P("cache", "tp", None),
            P("cache", None, "tp"),
            P("cache", None, "tp"),
            P("cache", None),
        ),
        out_specs=P("cache", "tp", None),
        check_vma=False,
    )
```

```python
import functools

import jax
import jax.numpy as jnp
import numpy as np
from jax import lax
from jax.experimental import pallas as pl
from jax.experimental.pallas import tpu as pltpu
from jax.sharding import PartitionSpec as P

HD = 128
EXTRA = 8
ROWS = 16
LOG2E = 1.4426950408889634
LARGE = 1e30
VMEM = pltpu.CompilerParams(vmem_limit_bytes=48 * 1024 * 1024)


def whole(shape):
    return pl.BlockSpec(shape, lambda *_: (0,) * len(shape))


def cut_bands(cache_keys, cache_values, lists, parts):
    owned, plen, width = cache_keys.shape
    half = parts // 2
    rows = owned * ROWS
    top = lists.shape[1]
    pieces = 1
    part = plen // pieces

    def kernel(lists_ref, k_ref, v_ref, out_ref, note_ref, list_buf, bufs, list_sem, sems):
        list_copy = pltpu.make_async_copy(lists_ref, list_buf, list_sem)
        list_copy.start()
        copies = {}
        for i in range(owned):
            for side, ref in enumerate((k_ref, v_ref)):
                for n in range(pieces):
                    at = pl.ds(n * part, part)
                    copy = pltpu.make_async_copy(ref.at[i, at], bufs.at[side, i, at], sems.at[side, i, n])
                    copy.start()
                    copies[side, i, n] = copy
        list_copy.wait()
        lane = lax.broadcasted_iota(jnp.int32, (top, width), 1)
        spread = lax.rem(lane, top) == lax.broadcasted_iota(jnp.int32, (top, width), 0)
        note = jnp.dot(
            list_buf[...].astype(jnp.bfloat16), spread.astype(jnp.bfloat16), preferred_element_type=jnp.float32
        )
        note_ref[...] = jnp.broadcast_to(note, (ROWS, width)).astype(note_ref.dtype)
        for i in range(owned):
            at = slice(i * ROWS, (i + 1) * ROWS)
            for side in range(2):
                for n in range(pieces):
                    copies[side, i, n].wait()
                out_ref[side * half : (side + 1) * half, at] = bufs[side, i].reshape(half, ROWS, width)

    return pl.pallas_call(
        kernel,
        in_specs=[pl.BlockSpec(memory_space=pltpu.HBM)] * 3,
        out_specs=[pl.BlockSpec(memory_space=pltpu.VMEM)] * 2,
        scratch_shapes=[
            pltpu.VMEM(lists.shape, lists.dtype),
            pltpu.VMEM((2, owned, plen, width), cache_keys.dtype),
            pltpu.SemaphoreType.DMA,
            pltpu.SemaphoreType.DMA((2, owned, pieces)),
        ],
        out_shape=[
            jax.ShapeDtypeStruct((parts, rows + EXTRA, width), cache_keys.dtype),
            jax.ShapeDtypeStruct((ROWS, width), cache_keys.dtype),
        ],
        compiler_params=pltpu.CompilerParams(vmem_limit_bytes=40 * 1024 * 1024),
        name="cut_bands",
    )(
        pltpu.with_memory_space_constraint(lists, pltpu.HBM),
        pltpu.with_memory_space_constraint(cache_keys, pltpu.HBM),
        pltpu.with_memory_space_constraint(cache_values, pltpu.HBM),
    )


def pick_rows(bands, lists, owned, top):
    parts, _, width = bands.shape
    each = lists.shape[1] // top
    assert owned & (owned - 1) == 0
    shift = owned.bit_length() - 1

    steps = 8
    share = parts // steps

    def kernel(lists_ref, bands_ref, out_ref, buf, sems):
        def one(d, carry):
            found = []
            for j in range(top):
                passage = lists_ref[lax.div(d, each), lax.rem(d, each) * top + j]
                at = pl.multiple_of(lax.bitwise_and(passage, owned - 1) * ROWS, ROWS)
                found.append(bands_ref[lax.shift_right_logical(passage, shift), pl.ds(at, ROWS)])
            for j in range(top):
                buf[d, j] = found[j]
            return carry

        copies = []
        for step in range(steps):
            lax.fori_loop(step * share, (step + 1) * share, one, 0, unroll=8)
            at = pl.ds(step * share, share)
            copies.append(pltpu.make_async_copy(buf.at[at], out_ref.at[at], sems.at[step]))
            copies[-1].start()
        for copy in copies:
            copy.wait()

    return pl.pallas_call(
        kernel,
        in_specs=[pl.BlockSpec(memory_space=pltpu.SMEM), pl.BlockSpec(memory_space=pltpu.VMEM)],
        out_specs=pl.BlockSpec(memory_space=pl.ANY),
        scratch_shapes=[
            pltpu.VMEM((parts, top, ROWS, width), bands.dtype),
            pltpu.SemaphoreType.DMA((steps,)),
        ],
        out_shape=jax.ShapeDtypeStruct((parts, top, ROWS, width), bands.dtype),
        compiler_params=VMEM,
        name="pick_rows",
    )(lists, bands)


def cut_heads(query, qkeys, qvalues, me, tp):
    tokens, width = query.shape[0], query.shape[1] // tp
    small = qkeys.shape[1] // tp

    def kernel(me_ref, q_ref, k_ref, v_ref, *outs):
        for k in range(tp):
            to = lax.rem(me_ref[0] + k, tp)
            big = pl.ds(pl.multiple_of(to * width, width), width)
            own = pl.ds(pl.multiple_of(to * small, small), small)
            outs[k][:, :width] = q_ref[:, big]
            outs[k][:, width : width + small] = k_ref[:, own]
            outs[k][:, width + small :] = v_ref[:, own]

    total = width + 2 * small
    return pl.pallas_call(
        kernel,
        grid_spec=pltpu.PrefetchScalarGridSpec(
            num_scalar_prefetch=1,
            grid=(1,),
            in_specs=[whole(query.shape), whole(qkeys.shape), whole(qvalues.shape)],
            out_specs=[whole((tokens, total))] * tp,
        ),
        out_shape=[jax.ShapeDtypeStruct((tokens, total), query.dtype)] * tp,
        compiler_params=VMEM,
        name="cut_heads",
    )(me, query, qkeys, qvalues)


def attend(parts_q, received, me, group):
    tp = len(parts_q)
    tokens, total = parts_q[0].shape
    qlen = tp * tokens
    width = group * HD
    bands, top, rows, _ = received.shape
    half = bands // 2
    keys_n = half * top * rows
    all_n = keys_n + qlen
    chunk = 512
    span = 2048
    factor = HD ** (-0.5) * LOG2E
    dims = (((1,), (1,)), ((), ()))

    def lane_max(s, most):
        pieces = [s[:, i : i + HD] for i in range(0, s.shape[1], HD)]
        return functools.reduce(jnp.maximum, pieces if most is None else [most] + pieces)

    def kernel(me_ref, *refs):
        q_refs = refs[:tp]
        k_ref, v_ref, out_ref, scores, values = refs[tp:]
        mine = me_ref[0]
        values[:, HD:] = jnp.ones((all_n, HD), values.dtype)
        values[:keys_n, :HD] = v_ref[...].reshape(keys_n, HD)
        for k in range(tp):
            values[keys_n + k * tokens : keys_n + (k + 1) * tokens, :HD] = q_refs[k][:, width + HD :]

        def position(axis):
            index = lax.broadcasted_iota(jnp.int32, (qlen, qlen), axis)
            owner = lax.bitwise_and(mine - index // tokens + tp, tp - 1)
            return owner * tokens + lax.rem(index, tokens)

        sees = position(0) >= position(1)
        own_keys = jnp.concatenate([q_refs[k][:, width : width + HD] for k in range(tp)], axis=0)

        def columns(g):
            return pl.ds(pl.multiple_of(g * HD, HD), HD)

        def queries(at):
            return jnp.concatenate([q_refs[k][:, at] for k in range(tp)], axis=0)

        def own_scores(q):
            return jnp.where(sees, lax.dot_general(q, own_keys, dims, preferred_element_type=jnp.float32), -jnp.inf)

        def listed_scores(q, c):
            keys = k_ref[c // (top * rows) : (c + chunk) // (top * rows)].reshape(chunk, HD)
            return lax.dot_general(q, keys, dims, preferred_element_type=jnp.float32)

        def weigh(s, m):
            return jnp.exp2((s - m) * factor).astype(values.dtype)

        def add_up(w, lo):
            return jnp.dot(w, values[lo : lo + w.shape[1]], preferred_element_type=jnp.float32)

        def store(at, sums):
            o = (sums[:, :HD] / sums[:, HD:]).astype(out_ref.dtype)
            for k in range(tp):
                owner = lax.bitwise_and(mine - k + tp, tp - 1)
                out_ref[owner, :, at] = o[k * tokens : (k + 1) * tokens]

        def begin(g):
            q = queries(slice(g * HD, (g + 1) * HD))
            s = own_scores(q)
            return q, s, jnp.max(lane_max(s, None), axis=1, keepdims=True)

        following = begin(0)
        too_large = jnp.zeros((qlen, HD), jnp.float32)
        for g in range(group):
            q, s, m = following
            sums = add_up(weigh(s, m), keys_n)
            for lo in range(0, keys_n, span):
                w = [weigh(listed_scores(q, c), m) for c in range(lo, lo + span, chunk)]
                sums = sums + add_up(jnp.concatenate(w, axis=1), lo)
                if lo == keys_n // 2 and g + 1 < group:
                    following = begin(g + 1)
            too_large = jnp.maximum(too_large, jnp.where(sums[:, HD:] < LARGE, 0.0, 1.0))
            store(slice(g * HD, (g + 1) * HD), sums)

        @pl.when(jnp.max(too_large) > 0.0)
        def _():
            def again(g, carry):
                q = queries(columns(g))
                s = own_scores(q)
                scores[:, keys_n:] = s
                most = lane_max(s, None)
                for c in range(0, keys_n, chunk):
                    s = listed_scores(q, c)
                    scores[:, c : c + chunk] = s
                    most = lane_max(s, most)
                m = jnp.max(most, axis=1, keepdims=True)
                sums = add_up(weigh(scores[:, keys_n:], m), keys_n)
                for c in range(0, keys_n, chunk):
                    sums = sums + add_up(weigh(scores[:, c : c + chunk], m), c)
                store(columns(g), sums)
                return carry

            lax.fori_loop(0, group, again, 0)

    return pl.pallas_call(
        kernel,
        grid_spec=pltpu.PrefetchScalarGridSpec(
            num_scalar_prefetch=1,
            grid=(1,),
            in_specs=[whole((tokens, total))] * tp
            + [
                pl.BlockSpec((half, top, rows, HD), lambda s, *_: (0, 0, 0, 0)),
                pl.BlockSpec((half, top, rows, HD), lambda s, *_: (1, 0, 0, 0)),
            ],
            out_specs=whole((tp, tokens, width)),
            scratch_shapes=[
                pltpu.VMEM((qlen, all_n), jnp.float32),
                pltpu.VMEM((all_n, 2 * HD), jnp.bfloat16),
            ],
        ),
        out_shape=jax.ShapeDtypeStruct((tp, tokens, width), jnp.bfloat16),
        compiler_params=VMEM,
        cost_estimate=pl.CostEstimate(
            flops=4 * group * qlen * all_n * HD,
            bytes_accessed=2 * keys_n * HD * 2,
            transcendentals=group * qlen * all_n,
        ),
        name="attend",
    )(me, *parts_q, received, received)


def join_heads(back):
    groups, tokens, width = back.shape
    half = tokens // 2

    def kernel(in_ref, out_ref, sems):
        copies = [
            pltpu.make_async_copy(
                in_ref.at[g, pl.ds(n * half, half)],
                out_ref.at[0, pl.ds(n * half, half), pl.ds(g * width, width)],
                sems.at[g, n],
            )
            for g in range(groups)
            for n in range(2)
        ]
        for copy in copies:
            copy.start()
        for copy in copies:
            copy.wait()

    return pl.pallas_call(
        kernel,
        in_specs=[pl.BlockSpec(memory_space=pltpu.VMEM)],
        out_specs=pl.BlockSpec(memory_space=pl.ANY),
        scratch_shapes=[pltpu.SemaphoreType.DMA((groups, 2))],
        out_shape=jax.ShapeDtypeStruct((1, tokens, groups * width), back.dtype),
        compiler_params=VMEM,
        name="join_heads",
    )(back)


def solution(mesh):
    parts, tp = mesh.shape["cache"], mesh.shape["tp"]

    def local(query, qkeys, qvalues, cache_keys, cache_values, lists):
        at_tp = lax.axis_index("tp").reshape(1).astype(jnp.int32)
        owned = cache_keys.shape[0]
        group = query.shape[2] // qkeys.shape[2]

        top = lists.shape[1]
        bands, note = cut_bands(cache_keys, cache_values, lists, parts)
        bands = bands.at[:, owned * ROWS :].set(note[None, :EXTRA])
        bands = lax.all_to_all(bands, "cache", split_axis=0, concat_axis=0, tiled=True)
        lanes = bands.shape[2]
        each = lanes // top
        mine = np.arange(parts)[:, None] % each == np.arange(lanes)[None, :] // top
        seen = jnp.where(mine, bands[:, owned * ROWS], 0).astype(jnp.int32).reshape(parts // each, each, lanes).sum(1)
        cuts = cut_heads(query[0], qkeys[0], qvalues[0], at_tp, tp)
        parts_q = [cuts[0]] + [
            lax.ppermute(cuts[k], "tp", [(d, (d + k) % tp) for d in range(tp)]) for k in range(1, tp)
        ]
        picked = pick_rows(bands, seen, owned, top)
        received = lax.all_to_all(picked, "cache", split_axis=0, concat_axis=0, tiled=True)
        result = attend(parts_q, received, at_tp, group)
        back = lax.all_to_all(result, "tp", split_axis=0, concat_axis=0, tiled=True)
        return join_heads(back)

    return jax.shard_map(
        local,
        mesh=mesh,
        in_specs=(
            P("cache", "tp", None),
            P("cache", "tp", None),
            P("cache", "tp", None),
            P("cache", None, "tp"),
            P("cache", None, "tp"),
            P("cache", None),
        ),
        out_specs=P("cache", "tp", None),
        check_vma=False,
    )
```
